256 devices in a mesh: seq: 64 (over x, z, core), head: 4 (over y).
Axes of the slice: x: 4, y: 4, z: 8, core: 2. Of those that a mesh axis runs over, the one named last changes fastest.
Arguments:
- image_input_rows: bfloat16 [8192, 3072], P(('seq', 'head')), may hold values from -6 to 6
- adapter_down_weight: bfloat16 [3072, 64], replicated, may hold values from -0.109375 to 0.109375
- adapter_up_weight: bfloat16 [64, 1536], replicated, may hold values from -0.75 to 0.75
- image_query_rows: bfloat16 [8192, 1536], P(('seq', 'head')), may hold values from -72 to 72
- image_key_rows: bfloat16 [8192, 1536], P(('seq', 'head')), may hold values from -4 to 4
- image_value_codes: int32 [8192, 1536], P(('seq', 'head')), may hold values from -127 to 127
- value_fraction: bfloat16 [8192, 1536], P(('seq', 'head')), may hold values from -0.5 to 0.5
- value_step_sizes: float32 [8, 12], replicated, may hold values from 0.004 to 0.03
- timestep_group: int32 [1000], replicated, may hold values from 0 to 7
- timestep: int32 [1], replicated, may hold values from 0 to 999
- image_output_grad: bfloat16 [8192, 1536], P(('seq', 'head')), may hold values from -1960 to 1960
- text_query_rows: bfloat16 [512, 1536], P(None, 'head'), may hold values from -4 to 4
- text_key_rows: bfloat16 [512, 1536], P(None, 'head'), may hold values from -4 to 4
- text_value_rows: bfloat16 [512, 1536], P(None, 'head'), may hold values from -4 to 4
- text_output_grad: bfloat16 [512, 1536], P(None, 'head'), may hold values from -512 to 512
Outputs:
- dq_img: bfloat16 [8192, 1536], P(('seq', 'head'))
- dk_img: bfloat16 [8192, 1536], P(('seq', 'head'))
- image_value_grad: bfloat16 [8192, 1536], P(('seq', 'head'))
- dq_txt: bfloat16 [512, 1536], P('seq', 'head')
- dk_txt: bfloat16 [512, 1536], P('seq', 'head')
- dv_txt: bfloat16 [512, 1536], P('seq', 'head')
- grad_down: float32 [3072, 64], replicated
- grad_up: float32 [64, 1536], replicated
- grad_steps: float32 [8, 12], replicated
The draws below stay inside these ranges and needn't reach their ends.
All inputs are finite; a program needn't handle non-finite values.
Results may differ from the reference program's by a relative error of at most 0.013.
Values may be sent and summed in bfloat16 or wider, within the bound.
No kernel may reach another device: no remote copies, remote signals or barrier semaphores. Data moves between devices by JAX's collectives and lax.ppermute only.
A program may use at most 128 MiB of HBM per device.

```python
import math
import jax
import jax.numpy as jnp
from jax import lax

MODEL_WIDTH = 3072
HEAD_SIZE = 128
HEAD_TOTAL = 12
ADAPTER_RANK = 64
TXT = 512
QMAX = 127
SLOTS = 8
TSTEPS = 1000
IMG = 8192


def shared_keys(key):
    return jax.random.truncated_normal(key, -3.0, 3.0, (IMG, HEAD_TOTAL * HEAD_SIZE), jnp.float32)


def draw_image_key_rows(key, part):
    shared = shared_keys(key)
    return shared.astype(jnp.bfloat16)


def draw_image_query_rows(key, part):
    key = jax.random.fold_in(key, 23)
    first_key = jax.random.fold_in(key, 0)
    drawn = jnp.clip(jax.random.normal(first_key, (IMG, HEAD_TOTAL * HEAD_SIZE), jnp.float32), -4.0, 4.0)
    return drawn.astype(jnp.bfloat16)


def draw_image_output_grad(key, part):
    key = jax.random.fold_in(key, 37)
    rising = jnp.arange(IMG, dtype=jnp.float32)[:, None] / IMG
    drawn = jnp.clip(jax.random.normal(key, (IMG, HEAD_TOTAL * HEAD_SIZE), jnp.float32), -4.0, 4.0)
    return (128.0 * (1.0 + 2.0 * rising) * drawn).astype(jnp.bfloat16)


def with_ends(entries, rng, low, largest):
    place = [jax.random.randint(jax.random.fold_in(rng, axis), (), 0, length) for axis, length in enumerate(entries.shape)]
    longest = entries.shape.index(max(entries.shape))
    next_to = place[:longest] + [(place[longest] + 1) % entries.shape[longest]] + place[longest + 1:]
    return entries.at[tuple(place)].set(low).at[tuple(next_to)].set(largest)


def shard_levels(key, extent, cuts, smallest, top_value):
    loudness, own = 1.0, jax.random.fold_in(key, 6)
    for dim, blocks in cuts:
        heights = jnp.exp(jax.random.uniform(jax.random.fold_in(own, dim), (blocks,), jnp.float32, smallest / len(cuts), top_value / len(cuts)))
        loudness = loudness * jnp.repeat(heights, extent[dim] // blocks).reshape([-1 if axis == dim else 1 for axis in range(len(extent))])
    return loudness


def bell_draw(rng, dims, spread, limit, shards=(), kind=jnp.bfloat16):
    level = shard_levels(rng, dims, shards, -0.22, 0.18) if shards else 1.0
    values = jax.random.normal(rng, dims, jnp.float32) * spread * level
    return jnp.minimum(jnp.maximum(values, -limit), limit).astype(kind)


def setup_inputs(seed: int = 0) -> dict:
    splits = jax.random.split(jax.random.key(seed), 16)
    return {
        "image_input_rows": bell_draw(splits[0], (IMG, MODEL_WIDTH), 1.0, 6.0, ((0, 256),)),
        "adapter_down_weight": bell_draw(splits[1], (MODEL_WIDTH, ADAPTER_RANK), MODEL_WIDTH ** -0.5, 0.109375),
        "adapter_up_weight": bell_draw(splits[2], (ADAPTER_RANK, HEAD_TOTAL * HEAD_SIZE), ADAPTER_RANK ** -0.5, 0.75),
        "image_query_rows": draw_image_query_rows(jax.random.fold_in(splits[15], 71), 0),
        "image_key_rows": draw_image_key_rows(jax.random.fold_in(splits[15], 71), 0),
        "image_value_codes": with_ends(jax.random.randint(splits[5], (IMG, HEAD_TOTAL * HEAD_SIZE), -QMAX, QMAX + 1), jax.random.fold_in(splits[5], 1), -QMAX, QMAX).astype(jnp.int32),
        "value_fraction": jnp.clip(jax.random.uniform(splits[6], (IMG, HEAD_TOTAL * HEAD_SIZE), jnp.float32, -0.5, 0.5) * shard_levels(splits[6], (IMG, HEAD_TOTAL * HEAD_SIZE), ((0, 256),), -0.4, 0.0), -0.5, 0.5).astype(jnp.bfloat16),
        "value_step_sizes": jnp.clip(jnp.exp(jax.random.uniform(splits[7], (SLOTS, HEAD_TOTAL), jnp.float32, math.log(0.004), math.log(0.03))), 0.004, 0.03),
        "timestep_group": with_ends(jax.random.randint(splits[8], (TSTEPS,), 0, SLOTS), jax.random.fold_in(splits[8], 1), 0, SLOTS - 1).astype(jnp.int32),
        "timestep": jax.random.randint(splits[9], (1,), 0, TSTEPS).astype(jnp.int32),
        "image_output_grad": draw_image_output_grad(jax.random.fold_in(splits[15], 71), 0),
        "text_query_rows": bell_draw(splits[11], (TXT, HEAD_TOTAL * HEAD_SIZE), 1.0, 4.0, ((1, 4),)),
        "text_key_rows": bell_draw(splits[12], (TXT, HEAD_TOTAL * HEAD_SIZE), 1.0, 4.0, ((1, 4),)),
        "text_value_rows": bell_draw(splits[13], (TXT, HEAD_TOTAL * HEAD_SIZE), 1.0, 4.0, ((1, 4),)),
        "text_output_grad": bell_draw(splits[14], (TXT, HEAD_TOTAL * HEAD_SIZE), 128.0, 512.0, ((1, 4),)),
    }


unscale = 0.0078125


def head_major(rows):
    return rows.reshape(rows.shape[0], HEAD_TOTAL, HEAD_SIZE).transpose(1, 0, 2)


def token_major(heads):
    return heads.transpose(1, 0, 2).reshape(heads.shape[1], HEAD_TOTAL * HEAD_SIZE)


def reference(image_input_rows, adapter_down_weight, adapter_up_weight, image_query_rows, image_key_rows, image_value_codes, value_fraction, value_step_sizes, timestep_group, timestep, image_output_grad, text_query_rows, text_key_rows, text_value_rows, text_output_grad):
    slot_index = timestep_group[timestep[0]]
    step_row = value_step_sizes[slot_index]
    code_values = image_value_codes.astype(jnp.float32)
    v_img = (code_values * jnp.repeat(step_row, HEAD_SIZE)[None, :]).astype(jnp.bfloat16)
    queries = head_major(jnp.concatenate([image_query_rows, text_query_rows], axis=0))
    key_rows = head_major(jnp.concatenate([image_key_rows, text_key_rows], axis=0))
    value_rows = head_major(jnp.concatenate([v_img, text_value_rows], axis=0))
    out_grads = head_major(jnp.concatenate([image_output_grad, text_output_grad], axis=0))
    total_rows = IMG + TXT
    block_rows = math.gcd(total_rows, 512)
    scale = HEAD_SIZE ** -0.5

    def one_head(operands):
        query_head, key_head, value_head, grad_head = operands
        query_blocks = query_head.reshape(total_rows // block_rows, block_rows, HEAD_SIZE)
        grad_blocks = grad_head.reshape(total_rows // block_rows, block_rows, HEAD_SIZE)

        def one_block(carried, blocks):
            key_grad, value_grad = carried
            query_block, grad_block = blocks
            scores = jnp.dot(query_block, key_head.T, preferred_element_type=jnp.float32) * scale
            row_max = jnp.max(scores, axis=1, keepdims=True)
            log_sums = row_max + jnp.log(jnp.sum(jnp.exp(scores - row_max), axis=1, keepdims=True))
            probs = jnp.exp(scores - log_sums)
            dprobs = jnp.dot(grad_block, value_head.T, preferred_element_type=jnp.float32)
            deltas = jnp.sum(probs * dprobs, axis=1, keepdims=True)
            dscores = (probs * (dprobs - deltas)).astype(jnp.bfloat16)
            query_grad = jnp.dot(dscores, key_head, preferred_element_type=jnp.float32) * scale
            key_grad = key_grad + jnp.dot(dscores.T, query_block, preferred_element_type=jnp.float32) * scale
            value_grad = value_grad + jnp.dot(probs.astype(jnp.bfloat16).T, grad_block, preferred_element_type=jnp.float32)
            return (key_grad, value_grad), query_grad

        empty = jnp.zeros((total_rows, HEAD_SIZE), jnp.float32)
        (key_grad, value_grad), query_grad = lax.scan(one_block, (empty, empty), (query_blocks, grad_blocks))
        return query_grad.reshape(total_rows, HEAD_SIZE), key_grad, value_grad

    query_grad, key_grad, value_grad = lax.map(one_head, (queries, key_rows, value_rows, out_grads))
    query_grad = token_major(query_grad).astype(jnp.bfloat16)
    key_grad = token_major(key_grad).astype(jnp.bfloat16)
    value_grad = token_major(value_grad).astype(jnp.bfloat16)
    dv_quant = value_grad[:IMG]
    inside = jnp.abs(image_value_codes) < QMAX
    lsq_term = jnp.where(inside, -value_fraction.astype(jnp.float32), code_values)
    image_value_grad = jnp.where(inside, dv_quant, jnp.zeros_like(dv_quant))
    head_sums = jnp.sum((dv_quant.astype(jnp.float32) * lsq_term).reshape(IMG, HEAD_TOTAL, HEAD_SIZE), axis=(0, 2))
    slot_rows = jnp.arange(SLOTS, dtype=jnp.int32) == slot_index
    grad_steps = jnp.where(slot_rows[:, None], head_sums[None, :], 0.0) * (QMAX ** -0.5 * unscale)
    lowrank_gradient = jnp.dot(image_value_grad, adapter_up_weight.T, preferred_element_type=jnp.float32).astype(jnp.bfloat16)
    grad_down = jnp.dot(image_input_rows.T, lowrank_gradient, preferred_element_type=jnp.float32) * unscale
    lowrank_input = jnp.dot(image_input_rows, adapter_down_weight, preferred_element_type=jnp.float32).astype(jnp.bfloat16)
    grad_up = jnp.dot(lowrank_input.T, image_value_grad, preferred_element_type=jnp.float32) * unscale
    return (query_grad[:IMG], key_grad[:IMG], image_value_grad, query_grad[IMG:], key_grad[IMG:], value_grad[IMG:], grad_down, grad_up, grad_steps)
```

```python
import functools
import math

import jax
import jax.numpy as jnp
from jax import lax
from jax.experimental import pallas as pl
from jax.experimental.pallas import tpu as pltpu
from jax.sharding import Mesh
from jax.sharding import PartitionSpec as P

HEAD_SIZE = 128
QMAX = 127
UNSCALE = 0.0078125
SCALE = HEAD_SIZE ** -0.5
SCALE_LOG2 = SCALE * math.log2(math.e)

IMG_ROWS = 1024
TXT_ROWS = 64
ROWS = IMG_ROWS + TXT_ROWS
HEADS = 3
TILE = 512

BF16 = jnp.bfloat16
F32 = jnp.float32
NT = (((1,), (1,)), ((), ()))
NN = (((1,), (0,)), ((), ()))
TN = (((0,), (0,)), ((), ()))


def dot(a, b, dims):
    return lax.dot_general(a, b, dims, preferred_element_type=F32)


def query_tiles():
    return [(s, TILE) for s in range(0, IMG_ROWS, TILE)] + [(IMG_ROWS, TXT_ROWS)]


def load_rows(scratch, gathered, which, text):
    scratch[0:IMG_ROWS] = gathered[:, which].reshape(IMG_ROWS, HEAD_SIZE)
    scratch[IMG_ROWS:ROWS] = text[...]


def stat_kernel(gq, gk, qt, gt, kt, vt, out, k_s, v_s, q_s, g_s):
    h = pl.program_id(0)
    load_rows(k_s, gk, 0, kt)
    load_rows(v_s, gk, 1, vt)
    load_rows(q_s, gq, 0, qt)
    load_rows(g_s, gq, 1, gt)
    for s, n in query_tiles():
        st = dot(k_s[...], q_s[s:s + n], NT)
        m = jnp.max(st, axis=0, keepdims=True)
        e = jnp.exp2((st - m) * SCALE_LOG2)
        l = jnp.sum(e, axis=0, keepdims=True)
        dp = dot(v_s[...], g_s[s:s + n], NT)
        w = jnp.sum(e * dp, axis=0, keepdims=True)
        log_sum = m * SCALE_LOG2 + jnp.log2(l)
        delta = w / l
        rows = lax.broadcasted_iota(jnp.int32, (8, n), 0)
        old = jnp.where(h == 0, 0.0, out[:, s:s + n])
        out[:, s:s + n] = jnp.where(
            rows == 2 * h, log_sum, jnp.where(rows == 2 * h + 1, delta, old)
        )


def grad_kernel(gq, gk, qt, gt, kt, vt, stats, dq, dkv, k_s, v_s, q_s, g_s, p_s, d_s, st_s):
    h = pl.program_id(0)
    load_rows(k_s, gk, 0, kt)
    load_rows(v_s, gk, 1, vt)
    load_rows(q_s, gq, 0, qt)
    load_rows(g_s, gq, 1, gt)
    logs = stats[:, pl.ds(2 * h, 1), :]
    deltas = stats[:, pl.ds(2 * h + 1, 1), :]
    m = jnp.max(logs, axis=0)
    e = jnp.exp2(logs - m[None])
    l = jnp.sum(e, axis=0)
    st_s[0:1] = m + jnp.log2(l)
    st_s[1:2] = jnp.sum(e * deltas, axis=0) / l
    for s, n in query_tiles():
        st = dot(k_s[...], q_s[s:s + n], NT)
        p = jnp.exp2(st * SCALE_LOG2 - st_s[0:1, s:s + n])
        dp = dot(v_s[...], g_s[s:s + n], NT)
        ds = p * (dp - st_s[1:2, s:s + n])
        p_s[:, s:s + n] = p.astype(BF16)
        d_s[:, s:s + n] = ds.astype(BF16)
    dv = dot(p_s[...], g_s[...], NN)
    dk = dot(d_s[...], q_s[...], NN) * SCALE
    dqv = dot(d_s[...], k_s[...], TN) * SCALE
    blank = jnp.zeros((8, 8, HEAD_SIZE), F32)
    dkv[:, 0:128] = dk[:IMG_ROWS].astype(BF16).reshape(8, 128, HEAD_SIZE)
    dkv[:, 128:256] = dv[:IMG_ROWS].astype(BF16).reshape(8, 128, HEAD_SIZE)
    dkv[:, 256:272] = jnp.concatenate(
        [dk[IMG_ROWS:].reshape(8, 8, HEAD_SIZE), dv[IMG_ROWS:].reshape(8, 8, HEAD_SIZE)], axis=1
    ).astype(BF16)
    dq[:, 0:128] = dqv[:IMG_ROWS].astype(BF16).reshape(8, 128, HEAD_SIZE)
    dq[:, 128:144] = jnp.concatenate(
        [dqv[IMG_ROWS:].reshape(8, 8, HEAD_SIZE), blank], axis=1
    ).astype(BF16)


def row_specs():
    image = pl.BlockSpec((32, 2, 32, HEAD_SIZE), lambda h: (0, 0, 0, h))
    text = pl.BlockSpec((TXT_ROWS, HEAD_SIZE), lambda h: (0, h))
    return [image, image, text, text, text, text]


def row_scratch():
    return [pltpu.VMEM((ROWS, HEAD_SIZE), BF16)] * 4


def row_stats(*rows):
    return pl.pallas_call(
        stat_kernel,
        grid=(HEADS,),
        in_specs=row_specs(),
        out_specs=pl.BlockSpec((8, ROWS), lambda h: (0, 0)),
        out_shape=jax.ShapeDtypeStruct((8, ROWS), F32),
        scratch_shapes=row_scratch(),
        name="row_stats",
        compiler_params=pltpu.CompilerParams(vmem_limit_bytes=48 << 20),
        cost_estimate=pl.CostEstimate(
            flops=4 * HEADS * ROWS * ROWS * HEAD_SIZE,
            bytes_accessed=4 << 20,
            transcendentals=HEADS * ROWS * ROWS,
        ),
    )(*rows)


def row_grads(*operands):
    return pl.pallas_call(
        grad_kernel,
        grid=(HEADS,),
        in_specs=row_specs() + [pl.BlockSpec((8, 8, ROWS), lambda h: (0, 0, 0))],
        out_specs=[
            pl.BlockSpec((8, 144, HEAD_SIZE), lambda h: (0, 0, h)),
            pl.BlockSpec((8, 272, HEAD_SIZE), lambda h: (0, 0, h)),
        ],
        out_shape=[
            jax.ShapeDtypeStruct((8, 144, HEADS * HEAD_SIZE), BF16),
            jax.ShapeDtypeStruct((8, 272, HEADS * HEAD_SIZE), BF16),
        ],
        scratch_shapes=row_scratch()
        + [pltpu.VMEM((ROWS, ROWS), BF16)] * 2
        + [pltpu.VMEM((8, ROWS), F32)],
        name="row_grads",
        compiler_params=pltpu.CompilerParams(vmem_limit_bytes=56 << 20),
        cost_estimate=pl.CostEstimate(
            flops=10 * HEADS * ROWS * ROWS * HEAD_SIZE,
            bytes_accessed=8 << 20,
            transcendentals=HEADS * ROWS * ROWS,
        ),
    )(*operands)


def on_device(
    image_input_rows,
    adapter_down_weight,
    adapter_up_weight,
    image_query_rows,
    image_key_rows,
    image_value_codes,
    value_fraction,
    value_step_sizes,
    timestep_group,
    timestep,
    image_output_grad,
    text_query_rows,
    text_key_rows,
    text_value_rows,
    text_output_grad,
):
    slot_index = jnp.sum(
        jnp.where(
            jnp.arange(timestep_group.shape[0], dtype=jnp.int32) == timestep[0], timestep_group, 0
        )
    )
    slot_rows = jnp.arange(value_step_sizes.shape[0], dtype=jnp.int32) == slot_index
    step_row = jnp.sum(jnp.where(slot_rows[:, None], value_step_sizes, 0.0), axis=0)
    code_values = image_value_codes.astype(F32)
    v_dequant = (code_values * jnp.repeat(step_row, HEAD_SIZE)[None, :]).astype(BF16)
    inside = jnp.abs(image_value_codes) < QMAX
    lsq_term = jnp.where(inside, -value_fraction.astype(F32), code_values)

    groups = lax.axis_size("head")
    width = image_query_rows.shape[1] // groups

    def by_group(rows):
        return rows.reshape(rows.shape[0], groups, width).transpose(1, 0, 2)

    packed = jnp.stack(
        [
            by_group(image_query_rows),
            by_group(image_output_grad),
            by_group(image_key_rows),
            by_group(v_dequant),
        ],
        axis=1,
    )
    own = lax.all_to_all(packed, "head", split_axis=0, concat_axis=0, tiled=True)
    token_rows = image_query_rows.shape[0]

    def gather(part, axes):
        flat = part.reshape(groups * 2 * token_rows, width)
        whole = lax.all_gather(flat, axes, axis=0, tiled=True)
        return whole.reshape(-1, 2, token_rows, width)

    gq = gather(own[:, 0:2], "z")
    gk = gather(own[:, 2:4], ("x", "core"))

    x_size, z_size, core_size = lax.axis_size("x"), lax.axis_size("z"), lax.axis_size("core")
    share = text_query_rows.shape[0] // (x_size * z_size * core_size)

    def text_for_queries(rows):
        table = rows.reshape(x_size, z_size, core_size, share, width)
        table = lax.dynamic_index_in_dim(table, lax.axis_index("x"), 0, keepdims=False)
        table = lax.dynamic_index_in_dim(table, lax.axis_index("core"), 1, keepdims=False)
        return table.reshape(z_size * share, width)

    def text_for_keys(rows):
        table = rows.reshape(x_size, z_size, core_size, share, width)
        table = lax.dynamic_index_in_dim(table, lax.axis_index("z"), 1, keepdims=False)
        return table.reshape(x_size * core_size * share, width)

    rows = (
        gq,
        gk,
        text_for_queries(text_query_rows),
        text_for_queries(text_output_grad),
        text_for_keys(text_key_rows),
        text_for_keys(text_value_rows),
    )
    stats = row_stats(*rows)
    all_stats = lax.all_gather(stats, "z", axis=0)
    dq_part, dkv_part = row_grads(*rows, all_stats)

    dkv_part = lax.all_to_all(dkv_part, ("x", "core"), split_axis=0, concat_axis=0, tiled=True)
    dq_part = lax.all_to_all(dq_part, "z", split_axis=0, concat_axis=0, tiled=True)
    dkv = jnp.sum(dkv_part.astype(F32), axis=0).astype(BF16)
    dq = jnp.sum(dq_part.astype(F32), axis=0).astype(BF16)
    dq_txt = dq[128:136]
    dk_txt = dkv[256:264]
    dv_txt = dkv[264:272]
    back = jnp.stack(
        [
            dq[0:128].reshape(groups, token_rows, width),
            dkv[0:128].reshape(groups, token_rows, width),
            dkv[128:256].reshape(groups, token_rows, width),
        ],
        axis=1,
    )
    back = lax.all_to_all(back, "head", split_axis=0, concat_axis=0, tiled=True)
    back = back.transpose(1, 2, 0, 3).reshape(3, token_rows, groups * width)
    dq_img, dk_img, dv_quant = back[0], back[1], back[2]

    image_value_grad = jnp.where(inside, dv_quant, jnp.zeros_like(dv_quant))
    lowrank_gradient = jnp.einsum(
        "vg,zg->vz", image_value_grad, adapter_up_weight, preferred_element_type=F32
    ).astype(BF16)
    part_down = jnp.einsum(
        "td,tr->dr", image_input_rows, lowrank_gradient, preferred_element_type=F32
    )
    lowrank_input = jnp.dot(
        image_input_rows, adapter_down_weight, preferred_element_type=F32
    ).astype(BF16)
    part_up = jnp.einsum(
        "tr,tw->rw", lowrank_input, image_value_grad, preferred_element_type=F32
    )
    token_terms = (dv_quant.astype(F32) * lsq_term).reshape(
        token_rows, value_step_sizes.shape[1], HEAD_SIZE
    )
    total_down, total_up, step_sums = lax.psum(
        (part_down, part_up, jnp.sum(token_terms, axis=(0, 2))), ("x", "z", "core", "head")
    )
    grad_steps = jnp.where(slot_rows[:, None], step_sums[None, :], 0.0) * (QMAX ** (-0.5) * UNSCALE)
    return (
        dq_img,
        dk_img,
        image_value_grad,
        dq_txt,
        dk_txt,
        dv_txt,
        total_down * UNSCALE,
        total_up * UNSCALE,
        grad_steps,
    )


def solution(mesh):
    fine = Mesh(mesh.devices.reshape(4, 8, 2, 4), ("x", "z", "core", "head"))
    seq = ("x", "z", "core")
    tokens = P(seq + ("head",), None)
    heads = P(None, "head")
    return jax.shard_map(
        on_device,
        mesh=fine,
        in_specs=(
            tokens,
            P(),
            P(),
            tokens,
            tokens,
            tokens,
            tokens,
            P(),
            P(),
            P(),
            tokens,
            heads,
            heads,
            heads,
            heads,
        ),
        out_specs=(
            tokens,
            tokens,
            tokens,
            P(seq, "head"),
            P(seq, "head"),
            P(seq, "head"),
            P(),
            P(),
            P(),
        ),
        check_vma=False,
    )
```

```python
import functools
import math

import jax
import jax.numpy as jnp
from jax import lax
from jax.experimental import pallas as pl
from jax.experimental.pallas import tpu as pltpu
from jax.sharding import Mesh
from jax.sharding import PartitionSpec as P

HEAD_SIZE = 128
QMAX = 127
UNSCALE = 0.0078125
SCALE = HEAD_SIZE ** -0.5
SCALE_LOG2 = SCALE * math.log2(math.e)

OWN = 128
IMG_ROWS = 1024
TXT_ROWS = 64
ROWS = IMG_ROWS + TXT_ROWS
HEADS = 3
WIDTH = HEADS * HEAD_SIZE
TOKENS = 32
GROUPS = 4
RANK = 64
DOWN = 768
LANES = 1280
TILE = 512

BF16 = jnp.bfloat16
F32 = jnp.float32
NT = (((1,), (1,)), ((), ()))
NN = (((1,), (0,)), ((), ()))
TN = (((0,), (0,)), ((), ()))


def dot(a, b, dims):
    return lax.dot_general(a, b, dims, preferred_element_type=F32)


def shift(rows, axis, step):
    size = lax.axis_size(axis)
    return lax.ppermute(rows, axis, [(i, (i + step) % size) for i in range(size)])


def flip(rows, axis, bit):
    size = lax.axis_size(axis)
    return lax.ppermute(rows, axis, [(i, i ^ bit) for i in range(size)])


def smem():
    return pl.BlockSpec(memory_space=pltpu.SMEM)


def vmem():
    return pl.BlockSpec(memory_space=pltpu.VMEM)


def params():
    return pltpu.CompilerParams(vmem_limit_bytes=56 << 20)


def shape(dims, dtype=BF16):
    return jax.ShapeDtypeStruct(dims, dtype)


def wrap(index, size):
    return lax.rem(index, size)


def columns(group, width):
    return pl.ds(pl.multiple_of(group * width, HEAD_SIZE), width)


def pack_kernel(place, q, g, k, codes, *outs):
    y = place[3]
    for d in range(GROUPS):
        at = columns(wrap(y + d, GROUPS), WIDTH)
        outs[d][0] = q[:, at]
        outs[d][1] = g[:, at]
        outs[d][2] = k[:, at]
        outs[d][3] = codes[:, at].astype(F32).astype(BF16)


def pack_rows(place, *rows):
    return pl.pallas_call(
        pack_kernel,
        in_specs=[smem()] + [vmem()] * 4,
        out_specs=[vmem()] * GROUPS,
        out_shape=[shape((4, TOKENS, WIDTH))] * GROUPS,
        name="pack_rows",
        compiler_params=params(),
    )(place, *rows)


def pack_more_kernel(place, x, fraction, down, *outs):
    y = place[3]
    low = dot(x[...], down[...], NN).astype(BF16)
    blank = jnp.zeros((TOKENS, HEAD_SIZE - RANK), BF16)
    for d in range(GROUPS):
        group = wrap(y + d, GROUPS)
        outs[d][:, 0:DOWN] = x[:, columns(group, DOWN)]
        outs[d][:, DOWN:DOWN + WIDTH] = fraction[:, columns(group, WIDTH)]
        outs[d][:, DOWN + WIDTH:LANES] = jnp.concatenate([low, blank], axis=1)


def pack_more(place, *rows):
    return pl.pallas_call(
        pack_more_kernel,
        in_specs=[smem()] + [vmem()] * 3,
        out_specs=[vmem()] * GROUPS,
        out_shape=[shape((TOKENS, LANES))] * GROUPS,
        name="pack_more",
        compiler_params=params(),
    )(place, *rows)


def query_tiles():
    return [(s, TILE) for s in range(0, IMG_ROWS, TILE)] + [(IMG_ROWS, TXT_ROWS)]


PIECES = 9


def place_pieces(whole, pieces, z):
    for piece, step in zip(pieces[:7], (0, 7, 6, 5, 1, 2, 3)):
        start = pl.multiple_of(wrap(z + step, 8) * OWN, OWN)
        whole[pl.ds(start, OWN)] = piece[...]
    start = pl.multiple_of(wrap(z + 4, 8) * OWN, OWN)
    whole[pl.ds(start, OWN // 2)] = pieces[7][...]
    whole[pl.ds(start + OWN // 2, OWN // 2)] = pieces[8][...]


def stat_kernel(place, *refs):
    q_pieces, g_pieces = refs[:PIECES], refs[PIECES:2 * PIECES]
    gk, qt, gt, kt, vt, step, out, qa, ga, ka, va = refs[2 * PIECES:]
    h = pl.program_id(0)
    z = place[1]
    place_pieces(qa, q_pieces, z)
    place_pieces(ga, g_pieces, z)
    qa[IMG_ROWS:ROWS] = qt[...]
    ga[IMG_ROWS:ROWS] = gt[...]
    ka[0:IMG_ROWS] = gk[:, 0].reshape(IMG_ROWS, HEAD_SIZE)
    ka[IMG_ROWS:ROWS] = kt[...]
    codes = gk[:, 1].reshape(IMG_ROWS, HEAD_SIZE).astype(F32)
    va[0:IMG_ROWS] = (codes * step[...]).astype(BF16)
    va[IMG_ROWS:ROWS] = vt[...]
    for s, n in query_tiles():
        st = dot(ka[...], qa[s:s + n], NT)
        m = jnp.max(st, axis=0, keepdims=True)
        e = jnp.exp2((st - m) * SCALE_LOG2)
        l = jnp.sum(e, axis=0, keepdims=True)
        dp = dot(va[...], ga[s:s + n], NT)
        w = jnp.sum(e * dp, axis=0, keepdims=True)
        log_sum = m * SCALE_LOG2 + jnp.log2(l)
        delta = w / l
        rows = lax.broadcasted_iota(jnp.int32, (8, n), 0)
        old = jnp.where(h == 0, 0.0, out[:, s:s + n])
        out[:, s:s + n] = jnp.where(
            rows == 2 * h, log_sum, jnp.where(rows == 2 * h + 1, delta, old)
        )


def row_stats(place, q_pieces, g_pieces, gk, qt, gt, kt, vt, step):
    def piece(rows):
        return pl.BlockSpec((rows, HEAD_SIZE), lambda h: (0, h))

    pieces = [piece(OWN)] * 7 + [piece(OWN // 2)] * 2
    return pl.pallas_call(
        stat_kernel,
        grid=(HEADS,),
        in_specs=[smem()]
        + pieces
        + pieces
        + [pl.BlockSpec((32, 2, TOKENS, HEAD_SIZE), lambda h: (0, 0, 0, h))]
        + [piece(TXT_ROWS)] * 4
        + [piece(1)],
        out_specs=[pl.BlockSpec((8, ROWS), lambda h: (0, 0))] + [piece(ROWS)] * 4,
        out_shape=[shape((8, ROWS), F32)] + [shape((ROWS, WIDTH))] * 4,
        name="row_stats",
        compiler_params=params(),
        cost_estimate=pl.CostEstimate(
            flops=4 * HEADS * ROWS * ROWS * HEAD_SIZE,
            bytes_accessed=8 << 20,
            transcendentals=HEADS * ROWS * ROWS,
        ),
    )(place, *q_pieces, *g_pieces, gk, qt, gt, kt, vt, step)


def grad_kernel(
    place, qa, ga, ka, va, stats, dq, keep_v, send_v, keep_k, send_k, p_s, d_s, st_s, v_s, k_s
):
    h = pl.program_id(0)
    x, c = place[0], place[2]
    logs = stats[:, pl.ds(2 * h, 1), :]
    deltas = stats[:, pl.ds(2 * h + 1, 1), :]
    m = jnp.max(logs, axis=0)
    e = jnp.exp2(logs - m[None])
    l = jnp.sum(e, axis=0)
    st_s[0:1] = m + jnp.log2(l)
    st_s[1:2] = jnp.sum(e * deltas, axis=0) / l
    for s, n in query_tiles():
        st = dot(ka[...], qa[s:s + n], NT)
        p = jnp.exp2(st * SCALE_LOG2 - st_s[0:1, s:s + n])
        dp = dot(va[...], ga[s:s + n], NT)
        ds = p * (dp - st_s[1:2, s:s + n])
        p_s[:, s:s + n] = p.astype(BF16)
        d_s[:, s:s + n] = ds.astype(BF16)
    v_s[...] = dot(p_s[...], ga[...], NN)
    k_s[...] = dot(d_s[...], qa[...], NN) * SCALE
    dqv = dot(d_s[...], ka[...], TN) * SCALE
    dq[:, 0:OWN] = dqv[:IMG_ROWS].reshape(8, OWN, HEAD_SIZE)
    dq[:, OWN:OWN + 8] = dqv[IMG_ROWS:].reshape(8, 8, HEAD_SIZE)
    for d in range(4):
        for core, to_v, to_k in ((c, keep_v, keep_k), (1 - c, send_v, send_k)):
            chunk = wrap(x + d, 4) * 2 + core
            rows = pl.ds(pl.multiple_of(chunk * OWN, OWN), OWN)
            text = pl.ds(pl.multiple_of(IMG_ROWS + chunk * 8, 8), 8)
            to_v[d] = v_s[rows].astype(to_v.dtype)
            to_k[d, 0:OWN] = k_s[rows].astype(to_k.dtype)
            both = jnp.concatenate([k_s[text], v_s[text]], axis=0)
            to_k[d, OWN:OWN + 16] = both.astype(to_k.dtype)


def row_grads(place, *operands):
    def chunks(rows):
        return pl.BlockSpec((4, rows, HEAD_SIZE), lambda h: (0, 0, h))

    return pl.pallas_call(
        grad_kernel,
        grid=(HEADS,),
        in_specs=[smem()]
        + [pl.BlockSpec((ROWS, HEAD_SIZE), lambda h: (0, h))] * 4
        + [pl.BlockSpec((8, 8, ROWS), lambda h: (0, 0, 0))],
        out_specs=[pl.BlockSpec((8, OWN + 8, HEAD_SIZE), lambda h: (0, 0, h))]
        + [chunks(OWN), chunks(OWN), chunks(OWN + 16), chunks(OWN + 16)],
        out_shape=[
            shape((8, OWN + 8, WIDTH), F32),
            shape((4, OWN, WIDTH), F32),
            shape((4, OWN, WIDTH)),
            shape((4, OWN + 16, WIDTH), F32),
            shape((4, OWN + 16, WIDTH)),
        ],
        scratch_shapes=[pltpu.VMEM((ROWS, ROWS), BF16)] * 2
        + [pltpu.VMEM((8, ROWS), F32)]
        + [pltpu.VMEM((ROWS, HEAD_SIZE), F32)] * 2,
        name="row_grads",
        compiler_params=params(),
        cost_estimate=pl.CostEstimate(
            flops=10 * HEADS * ROWS * ROWS * HEAD_SIZE,
            bytes_accessed=12 << 20,
            transcendentals=HEADS * ROWS * ROWS,
        ),
    )(place, *operands)


def value_kernel(own, r1, r2, r3, codes, fraction, low_input, up, dv, low, up_part, steps):
    total = own[...] + r1[...].astype(F32) + r2[...].astype(F32) + r3[...].astype(F32)
    dv_quant = total.astype(BF16)
    dv[...] = dv_quant.reshape(GROUPS, TOKENS, WIDTH)
    code = codes[...].reshape(OWN, WIDTH).astype(F32)
    inside = jnp.abs(code) < QMAX
    rounded = dv_quant.astype(F32)
    image_grad = jnp.where(inside, rounded, 0.0).astype(BF16)
    low[...] = dot(image_grad, up[...], NT)
    up_part[...] = dot(low_input[...], image_grad, TN)
    terms = rounded * jnp.where(inside, -fraction[...].astype(F32), code)
    sums = jnp.sum(terms, axis=0, keepdims=True)
    lane = lax.broadcasted_iota(jnp.int32, (8, HEAD_SIZE), 1)
    row = lax.broadcasted_iota(jnp.int32, (8, HEAD_SIZE), 0)
    found = jnp.zeros((8, HEAD_SIZE), F32)
    for h in range(HEADS):
        head_sum = jnp.sum(sums[:, h * HEAD_SIZE:(h + 1) * HEAD_SIZE], axis=1, keepdims=True)
        found = found + jnp.where((lane == h) & (row == 0), head_sum, 0.0)
    steps[...] = found


def value_terms(*operands):
    return pl.pallas_call(
        value_kernel,
        in_specs=[vmem()] * 8,
        out_specs=[vmem()] * 4,
        out_shape=[
            shape((GROUPS, TOKENS, WIDTH)),
            shape((OWN, RANK), F32),
            shape((RANK, WIDTH), F32),
            shape((8, HEAD_SIZE), F32),
        ],
        name="value_terms",
        compiler_params=params(),
    )(*operands)


def adapter_kernel(place, low0, low1, low2, low3, x_rows, up_part, steps, keep, send, whole):
    x, c = place[0], place[2]
    total = low0[...]
    for d, part in ((1, low1), (2, low2), (3, low3)):
        cut = (GROUPS - d) * TOKENS
        total = total + jnp.concatenate([part[cut:], part[:cut]], axis=0)
    whole[:, 0:DOWN] = dot(total.astype(BF16), x_rows[...], TN)
    whole[:, DOWN:DOWN + WIDTH] = up_part[...]
    whole[:, DOWN + WIDTH:LANES] = jnp.zeros((RANK, HEAD_SIZE), F32)
    whole[0:8, DOWN + WIDTH:LANES] = steps[...]
    for d in range(4):
        for core, to in ((c, keep), (1 - c, send)):
            start = (core * 4 + wrap(x + d, 4)) * 8
            to[d] = whole[pl.ds(pl.multiple_of(start, 8), 8)]


def adapter_terms(place, *operands):
    return pl.pallas_call(
        adapter_kernel,
        in_specs=[smem()] + [vmem()] * 7,
        out_specs=[vmem()] * 2,
        out_shape=[shape((4, 8, LANES), F32)] * 2,
        scratch_shapes=[pltpu.VMEM((RANK, LANES), F32)],
        name="adapter_terms",
        compiler_params=params(),
    )(place, *operands)


def place_kernel(place, slot, mine, other, down, up, steps, down_s):
    x, c, y = place[0], place[2], place[3]
    slot_row = lax.broadcasted_iota(jnp.int32, (8, HEAD_SIZE), 0) == slot[0]
    lane = lax.broadcasted_iota(jnp.int32, (8, HEAD_SIZE), 1)
    row = lax.broadcasted_iota(jnp.int32, (8, HEAD_SIZE), 0)
    found = jnp.zeros((1, HEAD_SIZE), F32)
    for e in range(GROUPS):
        group = wrap(y + GROUPS - e, GROUPS)
        for core, part in ((c, mine), (1 - c, other)):
            for d in range(4):
                index = core * 4 + wrap(x + 4 - d, 4)
                rows = pl.ds(pl.multiple_of(index * 8, 8), 8)
                tile = part[e, d] * UNSCALE
                down_s[rows, columns(group, DOWN)] = tile[:, 0:DOWN]
                up[rows, columns(group, WIDTH)] = tile[:, DOWN:DOWN + WIDTH]
                last = tile[:, DOWN + WIDTH:LANES]
                for h in range(HEADS):
                    value = jnp.sum(jnp.where((lane == h) & (row == 0), last, 0.0), axis=0, keepdims=True)
                    value = jnp.sum(value, axis=1, keepdims=True)
                    hit = (lane[0:1] == group * HEADS + h) & (index == 0)
                    found = found + jnp.where(hit, value, 0.0)
    steps[...] = jnp.where(slot_row, found * QMAX ** -0.5, 0.0)
    down[...] = down_s[...].T


def place_totals(place, slot, mine, other):
    return pl.pallas_call(
        place_kernel,
        in_specs=[smem()] * 2 + [vmem()] * 2,
        out_specs=[vmem()] * 3,
        out_shape=[
            shape((GROUPS * DOWN, RANK), F32),
            shape((RANK, GROUPS * WIDTH), F32),
            shape((8, HEAD_SIZE), F32),
        ],
        scratch_shapes=[pltpu.VMEM((RANK, GROUPS * DOWN), F32)],
        name="place_totals",
        compiler_params=params(),
    )(place, slot, mine, other)


def place_rows_kernel(place, *refs):
    pieces, (codes, dk, dv) = refs[:GROUPS], refs[GROUPS:]
    y = place[3]
    for d in range(GROUPS):
        at = columns(wrap(y + d, GROUPS), WIDTH)
        dk[:, at] = pieces[d][0]
        inside = jnp.abs(codes[:, at]) < QMAX
        value = pieces[d][1].astype(F32)
        dv[:, at] = jnp.where(inside, value, 0.0).astype(BF16)


def place_rows(place, pieces, codes):
    return pl.pallas_call(
        place_rows_kernel,
        in_specs=[smem()] + [vmem()] * (GROUPS + 1),
        out_specs=[vmem()] * 2,
        out_shape=[shape((TOKENS, GROUPS * WIDTH))] * 2,
        name="place_rows",
        compiler_params=params(),
    )(place, *pieces, codes)


def place_one_kernel(place, *refs):
    pieces, dq = refs[:GROUPS], refs[GROUPS]
    y = place[3]
    for d in range(GROUPS):
        dq[:, columns(wrap(y + d, GROUPS), WIDTH)] = pieces[d][...]


def place_one(place, pieces):
    return pl.pallas_call(
        place_one_kernel,
        in_specs=[smem()] + [vmem()] * GROUPS,
        out_specs=vmem(),
        out_shape=shape((TOKENS, GROUPS * WIDTH)),
        name="place_one",
        compiler_params=params(),
    )(place, *pieces)


def ring_pieces(rows):
    half = rows.shape[0] // 2
    left = [shift(rows, "z", 1)]
    right = [shift(rows, "z", -1)]
    for _ in range(2):
        left.append(shift(left[-1], "z", 1))
        right.append(shift(right[-1], "z", -1))
    first = shift(left[-1][:half], "z", 1)
    second = shift(right[-1][half:], "z", -1)
    return [rows, *left, *right, first, second]


def to_groups(slots):
    return [slots[0]] + [shift(slots[d], "head", d) for d in range(1, GROUPS)]


def from_groups(slots):
    return [slots[0]] + [shift(slots[d], "head", -d) for d in range(1, GROUPS)]


def on_device(
    image_input_rows,
    adapter_down_weight,
    adapter_up_weight,
    image_query_rows,
    image_key_rows,
    image_value_codes,
    value_fraction,
    value_step_sizes,
    timestep_group,
    timestep,
    image_output_grad,
    text_query_rows,
    text_key_rows,
    text_value_rows,
    text_output_grad,
):
    x_index, z_index = lax.axis_index("x"), lax.axis_index("z")
    core_index, group_index = lax.axis_index("core"), lax.axis_index("head")
    place = jnp.stack([x_index, z_index, core_index, group_index]).astype(jnp.int32)

    slots = pack_rows(place, image_query_rows, image_output_grad, image_key_rows, image_value_codes)
    own = jnp.stack(to_groups(slots))
    q_own = own[:, 0].reshape(OWN, WIDTH)
    g_own = own[:, 1].reshape(OWN, WIDTH)
    codes_own = own[:, 3].reshape(OWN, WIDTH)
    key_flat = own[:, 2:4].reshape(2 * OWN, WIDTH)
    gk = lax.all_gather(key_flat, ("x", "core"), axis=0, tiled=True)
    gk = gk.reshape(8 * GROUPS, 2, TOKENS, WIDTH)
    q_pieces = ring_pieces(q_own)
    g_pieces = ring_pieces(g_own)

    slot_index = jnp.sum(
        jnp.where(
            jnp.arange(timestep_group.shape[0], dtype=jnp.int32) == timestep[0], timestep_group, 0
        )
    )
    slot_rows = jnp.arange(value_step_sizes.shape[0], dtype=jnp.int32) == slot_index
    step_row = jnp.sum(jnp.where(slot_rows[:, None], value_step_sizes, 0.0), axis=0)
    step = lax.dynamic_slice_in_dim(step_row, group_index * HEADS, HEADS, 0)
    step = jnp.repeat(step, HEAD_SIZE)[None, :]

    x_size, z_size, core_size = lax.axis_size("x"), lax.axis_size("z"), lax.axis_size("core")
    share = text_query_rows.shape[0] // (x_size * z_size * core_size)

    def text_for_queries(rows):
        table = rows.reshape(x_size, z_size, core_size, share, WIDTH)
        table = lax.dynamic_index_in_dim(table, x_index, 0, keepdims=False)
        table = lax.dynamic_index_in_dim(table, core_index, 1, keepdims=False)
        return table.reshape(z_size * share, WIDTH)

    def text_for_keys(rows):
        table = rows.reshape(x_size, z_size, core_size, share, WIDTH)
        table = lax.dynamic_index_in_dim(table, z_index, 1, keepdims=False)
        return table.reshape(x_size * core_size * share, WIDTH)

    stats, qa, ga, ka, va = row_stats(
        place,
        q_pieces,
        g_pieces,
        gk,
        text_for_queries(text_query_rows),
        text_for_queries(text_output_grad),
        text_for_keys(text_key_rows),
        text_for_keys(text_value_rows),
        step,
    )
    copies = jnp.broadcast_to(stats[None], (8, 8, ROWS))
    all_stats = lax.all_to_all(copies, "z", split_axis=0, concat_axis=0, tiled=True)

    more = to_groups(pack_more(place, image_input_rows, value_fraction, adapter_down_weight))
    more = jnp.concatenate(more, axis=0)
    x_rows = more[:, 0:DOWN]
    fraction_own = more[:, DOWN:DOWN + WIDTH]
    low_input = more[:, DOWN + WIDTH:DOWN + WIDTH + RANK]
    up_own = lax.dynamic_slice_in_dim(adapter_up_weight, group_index * WIDTH, WIDTH, 1)

    dq_part, keep_v, send_v, keep_k, send_k = row_grads(place, qa, ga, ka, va, all_stats)

    sum_v = keep_v + flip(send_v, "core", 1).astype(F32)
    low_v = sum_v.astype(BF16)
    arrived_v = [shift(low_v[d], "x", d) for d in range(1, 4)]
    dv_slots, low_part, up_part, steps_part = value_terms(
        sum_v[0], *arrived_v, codes_own, fraction_own, low_input, up_own
    )
    low_parts = [low_part] + [shift(low_part, "head", d) for d in range(1, GROUPS)]
    keep_a, send_a = adapter_terms(place, *low_parts, x_rows, up_part, steps_part)
    sum_a = keep_a + flip(send_a, "core", 1)
    total = sum_a[0]
    for d in range(1, 4):
        total = total + shift(sum_a[d], "x", d)
    for bit in (1, 2, 4):
        total = total + flip(total, "z", bit)
    by_x = jnp.stack([total] + [shift(total, "x", d) for d in range(1, 4)])
    by_group = jnp.stack([by_x] + [shift(by_x, "head", d) for d in range(1, GROUPS)])
    other = flip(by_group, "core", 1)
    grad_down, grad_up, grad_steps = place_totals(place, slot_index[None], by_group, other)
    grad_steps = grad_steps[:, :value_step_sizes.shape[1]]

    dq_own = lax.psum_scatter(
        dq_part.reshape(8 * (OWN + 8), WIDTH), "z", scatter_dimension=0, tiled=True
    )
    dq_own = dq_own.astype(BF16)

    sum_k = keep_k + flip(send_k, "core", 1).astype(F32)
    low_k = sum_k.astype(BF16)
    total_k = sum_k[0]
    for d in range(1, 4):
        total_k = total_k + shift(low_k[d], "x", d).astype(F32)
    total_k = total_k.astype(BF16)

    back = jnp.stack([total_k[:OWN].reshape(GROUPS, TOKENS, WIDTH), dv_slots], axis=1)
    dk_img, image_value_grad = place_rows(place, from_groups(back), image_value_codes)
    dq_img = place_one(place, from_groups(dq_own[:OWN].reshape(GROUPS, TOKENS, WIDTH)))
    return (
        dq_img,
        dk_img,
        image_value_grad,
        dq_own[OWN:OWN + 8],
        total_k[OWN:OWN + 8],
        total_k[OWN + 8:OWN + 16],
        grad_down,
        grad_up,
        grad_steps,
    )


def solution(mesh):
    fine = Mesh(mesh.devices.reshape(4, 8, 2, 4), ("x", "z", "core", "head"))
    seq = ("x", "z", "core")
    tokens = P(seq + ("head",), None)
    heads = P(None, "head")
    return jax.shard_map(
        on_device,
        mesh=fine,
        in_specs=(
            tokens,
            P(),
            P(),
            tokens,
            tokens,
            tokens,
            tokens,
            P(),
            P(),
            P(),
            tokens,
            heads,
            heads,
            heads,
            heads,
        ),
        out_specs=(
            tokens,
            tokens,
            tokens,
            P(seq, "head"),
            P(seq, "head"),
            P(seq, "head"),
            P(),
            P(),
            P(),
        ),
        check_vma=False,
    )
```

```python
import functools
import math

import jax
import jax.numpy as jnp
from jax import lax
from jax.experimental import pallas as pl
from jax.experimental.pallas import tpu as pltpu
from jax.sharding import Mesh
from jax.sharding import PartitionSpec as P

HEAD_SIZE = 128
QMAX = 127
UNSCALE = 0.0078125
SCALE = HEAD_SIZE ** -0.5
SCALE_LOG2 = SCALE * math.log2(math.e)

OWN = 128
IMG_ROWS = 1024
TXT_ROWS = 64
ROWS = IMG_ROWS + TXT_ROWS
HEADS = 3
WIDTH = HEADS * HEAD_SIZE
TOKENS = 32
GROUPS = 4
RANK = 64
DOWN = 768
LANES = 1280
LINE = 1152
TILE = 512

BF16 = jnp.bfloat16
F32 = jnp.float32
NT = (((1,), (1,)), ((), ()))
NN = (((1,), (0,)), ((), ()))
TN = (((0,), (0,)), ((), ()))


def dot(a, b, dims):
    return lax.dot_general(a, b, dims, preferred_element_type=F32)


def shift(rows, axis, step):
    size = lax.axis_size(axis)
    return lax.ppermute(rows, axis, [(i, (i + step) % size) for i in range(size)])


def flip(rows, axis, bit):
    size = lax.axis_size(axis)
    return lax.ppermute(rows, axis, [(i, i ^ bit) for i in range(size)])


def smem():
    return pl.BlockSpec(memory_space=pltpu.SMEM)


def vmem():
    return pl.BlockSpec(memory_space=pltpu.VMEM)


def params():
    return pltpu.CompilerParams(vmem_limit_bytes=56 << 20)


def shape(dims, dtype=BF16):
    return jax.ShapeDtypeStruct(dims, dtype)


def wrap(index, size):
    return lax.rem(index, size)


def columns(group, width):
    return pl.ds(pl.multiple_of(group * width, HEAD_SIZE), width)


def pack_kernel(place, q, g, k, codes, *outs):
    y = place[3]
    for d in range(GROUPS):
        at = columns(wrap(y + d, GROUPS), WIDTH)
        outs[d][0] = q[:, at]
        outs[d][1] = g[:, at]
        outs[d][2] = k[:, at]
        outs[d][3] = codes[:, at].astype(F32).astype(BF16)


def pack_rows(place, *rows):
    return pl.pallas_call(
        pack_kernel,
        in_specs=[smem()] + [vmem()] * 4,
        out_specs=[vmem()] * GROUPS,
        out_shape=[shape((4, TOKENS, WIDTH))] * GROUPS,
        name="pack_rows",
        compiler_params=params(),
    )(place, *rows)


def join_kernel(s0, s1, s2, s3, rows, keys):
    for d, slot in enumerate((s0, s1, s2, s3)):
        rows[d * TOKENS:(d + 1) * TOKENS] = slot[0]
        rows[OWN + d * TOKENS:OWN + (d + 1) * TOKENS] = slot[1]
        keys[2 * d * TOKENS:(2 * d + 1) * TOKENS] = slot[2]
        keys[(2 * d + 1) * TOKENS:(2 * d + 2) * TOKENS] = slot[3]


def join_slots(slots):
    return pl.pallas_call(
        join_kernel,
        in_specs=[vmem()] * GROUPS,
        out_specs=[vmem()] * 2,
        out_shape=[shape((2 * OWN, WIDTH))] * 2,
        name="join_slots",
        compiler_params=params(),
    )(*slots)


def pack_more_kernel(place, x, fraction, down_t, *outs):
    y = place[3]
    low = dot(x[...], down_t[...], NT).astype(BF16)
    blank = jnp.zeros((TOKENS, HEAD_SIZE - RANK), BF16)
    for d in range(GROUPS):
        group = wrap(y + d, GROUPS)
        outs[d][:, 0:DOWN] = x[:, columns(group, DOWN)]
        outs[d][:, DOWN:DOWN + WIDTH] = fraction[:, columns(group, WIDTH)]
        outs[d][:, DOWN + WIDTH:LANES] = jnp.concatenate([low, blank], axis=1)


def pack_more(place, *rows):
    return pl.pallas_call(
        pack_more_kernel,
        in_specs=[smem()] + [vmem()] * 3,
        out_specs=[vmem()] * GROUPS,
        out_shape=[shape((TOKENS, LANES))] * GROUPS,
        name="pack_more",
        compiler_params=params(),
    )(place, *rows)


def query_tiles():
    return [(s, TILE) for s in range(0, IMG_ROWS, TILE)] + [(IMG_ROWS, TXT_ROWS)]


PIECES = 9


def place_pieces(qa, ga, pieces, z):
    for piece, step in zip(pieces[:7], (0, 7, 6, 5, 1, 2, 3)):
        start = pl.multiple_of(wrap(z + step, 8) * OWN, OWN)
        qa[pl.ds(start, OWN)] = piece[0:OWN]
        ga[pl.ds(start, OWN)] = piece[OWN:2 * OWN]
    start = pl.multiple_of(wrap(z + 4, 8) * OWN, OWN)
    qa[pl.ds(start, OWN)] = pieces[7][...]
    ga[pl.ds(start, OWN)] = pieces[8][...]


def query_text(text, place):
    row = lax.broadcasted_iota(jnp.int32, (TXT_ROWS, 512), 0)
    column = lax.broadcasted_iota(jnp.int32, (TXT_ROWS, 512), 1)
    wanted = lax.shift_right_logical(row, 3) * 16 + lax.bitwise_and(row, 7)
    pick = jnp.where(column == wanted + place[0] * 128 + place[2] * 8, 1.0, 0.0).astype(BF16)
    return dot(pick, text[...], NN).astype(BF16)


def key_text(text, place):
    row = lax.broadcasted_iota(jnp.int32, (TXT_ROWS, 512), 0)
    column = lax.broadcasted_iota(jnp.int32, (TXT_ROWS, 512), 1)
    block = lax.shift_right_logical(row, 4) * 128 + lax.bitwise_and(row, 15)
    pick = jnp.where(column == block + place[1] * 16, 1.0, 0.0).astype(BF16)
    return dot(pick, text[...], NN).astype(BF16)


def rows_spec(rows):
    return pl.BlockSpec((rows, HEAD_SIZE), lambda h: (0, h))


def line_spec(copies):
    return pl.BlockSpec((copies, 2, LINE), lambda h: (0, 0, h))


def cost(matmuls, moved):
    return pl.CostEstimate(
        flops=2 * matmuls * HEADS * ROWS * ROWS * HEAD_SIZE,
        bytes_accessed=moved << 20,
        transcendentals=HEADS * ROWS * ROWS,
    )


def chunk_spec(rows):
    return pl.BlockSpec((4, rows, HEAD_SIZE), lambda h: (0, 0, h))


def stat_kernel(place, group, timestep, sizes, *refs):
    pieces = refs[:PIECES]
    gk, qt, gt, kt, vt, out, qa, ga, ka, va = refs[PIECES:]
    step = sizes[group[timestep[0]], place[3] * HEADS + pl.program_id(0)]
    place_pieces(qa, ga, pieces, place[1])
    qa[IMG_ROWS:ROWS] = query_text(qt, place)
    ga[IMG_ROWS:ROWS] = query_text(gt, place)
    ka[0:IMG_ROWS] = gk[:, 0].reshape(IMG_ROWS, HEAD_SIZE)
    ka[IMG_ROWS:ROWS] = key_text(kt, place)
    codes = gk[:, 1].reshape(IMG_ROWS, HEAD_SIZE).astype(F32)
    va[0:IMG_ROWS] = (codes * step).astype(BF16)
    va[IMG_ROWS:ROWS] = key_text(vt, place)
    for s, n in query_tiles():
        st = dot(ka[...], qa[s:s + n], NT)
        m = jnp.max(st, axis=0, keepdims=True)
        e = jnp.exp2((st - m) * SCALE_LOG2)
        l = jnp.sum(e, axis=0, keepdims=True)
        dp = dot(va[...], ga[s:s + n], NT)
        w = jnp.sum(e * dp, axis=0, keepdims=True)
        lines = jnp.concatenate([m * SCALE_LOG2 + jnp.log2(l), w / l], axis=0)
        out[:, :, s:s + n] = jnp.broadcast_to(lines[None], (8, 2, n))
    out[:, :, ROWS:LINE] = jnp.zeros((8, 2, LINE - ROWS), F32)


def row_stats(place, group, timestep, sizes, pieces, *operands):
    return pl.pallas_call(
        stat_kernel,
        grid=(HEADS,),
        in_specs=[smem()] * 4
        + [rows_spec(2 * OWN)] * 7
        + [rows_spec(OWN)] * 2
        + [pl.BlockSpec((32, 2, TOKENS, HEAD_SIZE), lambda h: (0, 0, 0, h))]
        + [rows_spec(512)] * 4,
        out_specs=[line_spec(8)] + [rows_spec(ROWS)] * 4,
        out_shape=[shape((8, 2, HEADS * LINE), F32)] + [shape((ROWS, WIDTH))] * 4,
        name="row_stats",
        compiler_params=params(),
        cost_estimate=cost(2, 8),
    )(place, group, timestep, sizes, *pieces, *operands)


def grad_kernel(place, qa, ga, ka, va, stats, dq, keep_v, send_v, keep_k, send_k, p_s, d_s, v_s, k_s):
    x, c = place[0], place[2]
    logs, parts = stats[:, 0], stats[:, 1]
    m = jnp.max(logs, axis=0, keepdims=True)
    e = jnp.exp2(logs - m)
    l = jnp.sum(e, axis=0, keepdims=True)
    log = m + jnp.log2(l)
    delta = jnp.sum(e * parts, axis=0, keepdims=True) / l
    for s, n in query_tiles():
        st = dot(ka[...], qa[s:s + n], NT)
        p = jnp.exp2(st * SCALE_LOG2 - log[:, s:s + n])
        dp = dot(va[...], ga[s:s + n], NT)
        p_s[:, s:s + n] = p.astype(BF16)
        d_s[:, s:s + n] = (p * (dp - delta[:, s:s + n])).astype(BF16)
    v_s[...] = dot(p_s[...], ga[...], NN)
    k_s[...] = dot(d_s[...], qa[...], NN) * SCALE
    dqv = dot(d_s[...], ka[...], TN) * SCALE
    blank = jnp.zeros((8, 8, HEAD_SIZE), F32)
    dq[:, 0:OWN] = dqv[:IMG_ROWS].astype(BF16).reshape(8, OWN, HEAD_SIZE)
    dq[:, OWN:OWN + 16] = jnp.concatenate(
        [dqv[IMG_ROWS:].reshape(8, 8, HEAD_SIZE), blank], axis=1
    ).astype(BF16)
    for d in range(4):
        for core, to_v, to_k in ((c, keep_v, keep_k), (1 - c, send_v, send_k)):
            chunk = wrap(x + d, 4) * 2 + core
            rows = pl.ds(pl.multiple_of(chunk * OWN, OWN), OWN)
            text = pl.ds(pl.multiple_of(IMG_ROWS + chunk * 8, 8), 8)
            to_v[d] = v_s[rows].astype(to_v.dtype)
            to_k[d, 0:OWN] = k_s[rows].astype(to_k.dtype)
            both = jnp.concatenate([k_s[text], v_s[text]], axis=0)
            to_k[d, OWN:OWN + 16] = both.astype(to_k.dtype)


def row_grads(place, *operands):
    return pl.pallas_call(
        grad_kernel,
        grid=(HEADS,),
        in_specs=[smem()] + [rows_spec(ROWS)] * 4 + [line_spec(8)],
        out_specs=[pl.BlockSpec((8, OWN + 16, HEAD_SIZE), lambda h: (0, 0, h))]
        + [chunk_spec(OWN), chunk_spec(OWN), chunk_spec(OWN + 16), chunk_spec(OWN + 16)],
        out_shape=[
            shape((8, OWN + 16, WIDTH)),
            shape((4, OWN, WIDTH), F32),
            shape((4, OWN, WIDTH)),
            shape((4, OWN + 16, WIDTH), F32),
            shape((4, OWN + 16, WIDTH)),
        ],
        scratch_shapes=[pltpu.VMEM((ROWS, ROWS), BF16)] * 2
        + [pltpu.VMEM((ROWS, HEAD_SIZE), F32)] * 2,
        name="row_grads",
        compiler_params=params(),
        cost_estimate=cost(5, 12),
    )(place, *operands)


def value_kernel(own, r1, r2, r3, codes, more, up, dv, low, up_part, steps):
    total = own[...] + r1[...].astype(F32) + r2[...].astype(F32) + r3[...].astype(F32)
    dv_quant = total.astype(BF16)
    dv[...] = dv_quant.reshape(GROUPS, TOKENS, WIDTH)
    pairs = codes[...].reshape(GROUPS, 2, TOKENS, WIDTH)
    code = pairs[:, 1].reshape(OWN, WIDTH).astype(F32)
    inside = jnp.abs(code) < QMAX
    rounded = dv_quant.astype(F32)
    image_grad = jnp.where(inside, rounded, 0.0).astype(BF16)
    low[...] = dot(image_grad, up[...], NT).astype(BF16)
    low_input = more[:, DOWN + WIDTH:DOWN + WIDTH + RANK]
    fraction = more[:, DOWN:DOWN + WIDTH].astype(F32)
    up_part[...] = dot(low_input, image_grad, TN)
    terms = rounded * jnp.where(inside, -fraction, code)
    sums = jnp.sum(terms, axis=0, keepdims=True)
    lane = lax.broadcasted_iota(jnp.int32, (8, HEAD_SIZE), 1)
    row = lax.broadcasted_iota(jnp.int32, (8, HEAD_SIZE), 0)
    found = jnp.zeros((8, HEAD_SIZE), F32)
    for h in range(HEADS):
        head_sum = jnp.sum(sums[:, h * HEAD_SIZE:(h + 1) * HEAD_SIZE], axis=1, keepdims=True)
        found = found + jnp.where((lane == h) & (row == 0), head_sum, 0.0)
    steps[...] = found


def value_terms(*operands):
    return pl.pallas_call(
        value_kernel,
        in_specs=[vmem()] * 7,
        out_specs=[vmem()] * 4,
        out_shape=[
            shape((GROUPS, TOKENS, WIDTH)),
            shape((OWN, RANK)),
            shape((RANK, WIDTH), F32),
            shape((8, HEAD_SIZE), F32),
        ],
        name="value_terms",
        compiler_params=params(),
    )(*operands)


def adapter_kernel(place, low0, low1, low2, low3, more, up_part, steps, keep, send, whole):
    x, c = place[0], place[2]
    total = low0[...].astype(F32)
    for d, part in ((1, low1), (2, low2), (3, low3)):
        cut = (GROUPS - d) * TOKENS
        total = total + jnp.concatenate([part[cut:], part[:cut]], axis=0).astype(F32)
    whole[:, 0:DOWN] = dot(total.astype(BF16), more[:, 0:DOWN], TN)
    whole[:, DOWN:DOWN + WIDTH] = up_part[...]
    whole[:, DOWN + WIDTH:LANES] = jnp.zeros((RANK, HEAD_SIZE), F32)
    whole[0:8, DOWN + WIDTH:LANES] = steps[...]
    for d in range(4):
        for core, to in ((c, keep), (1 - c, send)):
            start = (core * 4 + wrap(x + d, 4)) * 8
            to[d] = whole[pl.ds(pl.multiple_of(start, 8), 8)].astype(to.dtype)


def adapter_terms(place, *operands):
    return pl.pallas_call(
        adapter_kernel,
        in_specs=[smem()] + [vmem()] * 7,
        out_specs=[vmem()] * 2,
        out_shape=[shape((4, 8, LANES), F32), shape((4, 8, LANES), F32)],
        scratch_shapes=[pltpu.VMEM((RANK, LANES), F32)],
        name="adapter_terms",
        compiler_params=params(),
    )(place, *operands)


def place_kernel(place, group_table, timestep, mine, other, down_t, up, steps):
    x, c, y = place[0], place[2], place[3]
    slot_row = lax.broadcasted_iota(jnp.int32, (8, HEAD_SIZE), 0) == group_table[timestep[0]]
    lane = lax.broadcasted_iota(jnp.int32, (8, HEAD_SIZE), 1)
    row = lax.broadcasted_iota(jnp.int32, (8, HEAD_SIZE), 0)
    found = jnp.zeros((1, HEAD_SIZE), F32)
    for e in range(GROUPS):
        group = wrap(y + GROUPS - e, GROUPS)
        for core, part in ((c, mine), (1 - c, other)):
            for d in range(4):
                index = core * 4 + wrap(x + 4 - d, 4)
                rows = pl.ds(pl.multiple_of(index * 8, 8), 8)
                tile = part[e, d].astype(F32) * UNSCALE
                down_t[rows, columns(group, DOWN)] = tile[:, 0:DOWN]
                up[rows, columns(group, WIDTH)] = tile[:, DOWN:DOWN + WIDTH]
                last = tile[:, DOWN + WIDTH:LANES]
                for h in range(HEADS):
                    value = jnp.sum(jnp.where((lane == h) & (row == 0), last, 0.0), axis=0, keepdims=True)
                    value = jnp.sum(value, axis=1, keepdims=True)
                    hit = (lane[0:1] == group * HEADS + h) & (index == 0)
                    found = found + jnp.where(hit, value, 0.0)
    steps[...] = jnp.where(slot_row, found * QMAX ** -0.5, 0.0)[:, 0:GROUPS * HEADS]


def place_totals(place, group_table, timestep, mine, other):
    return pl.pallas_call(
        place_kernel,
        in_specs=[smem()] * 3 + [vmem()] * 2,
        out_specs=[vmem()] * 3,
        out_shape=[
            shape((RANK, GROUPS * DOWN), F32),
            shape((RANK, GROUPS * WIDTH), F32),
            shape((8, GROUPS * HEADS), F32),
        ],
        name="place_totals",
        compiler_params=params(),
    )(place, group_table, timestep, mine, other)


def place_rows_kernel(place, *refs):
    pieces, (codes, q_tail, k_tail, dq, dk, dv, q_txt, k_txt, v_txt) = refs[:GROUPS], refs[GROUPS:]
    y = place[3]
    q_txt[...] = q_tail[OWN:OWN + 16].astype(F32)[0:8].astype(BF16)
    tail = k_tail[OWN:OWN + 16].astype(F32)
    k_txt[...] = tail[0:8].astype(BF16)
    v_txt[...] = tail[8:16].astype(BF16)
    for d in range(GROUPS):
        at = columns(wrap(y + d, GROUPS), WIDTH)
        dq[:, at] = pieces[d][0]
        dk[:, at] = pieces[d][1]
        inside = jnp.abs(codes[:, at]) < QMAX
        value = pieces[d][2].astype(F32)
        dv[:, at] = jnp.where(inside, value, 0.0).astype(BF16)


def place_rows(place, pieces, codes, q_tail, k_tail):
    return pl.pallas_call(
        place_rows_kernel,
        in_specs=[smem()] + [vmem()] * (GROUPS + 3),
        out_specs=[vmem()] * 6,
        out_shape=[shape((TOKENS, GROUPS * WIDTH))] * 3 + [shape((8, WIDTH))] * 3,
        name="place_rows",
        compiler_params=params(),
    )(place, *pieces, codes, q_tail, k_tail)


def ring_pieces(rows):
    half = rows.shape[0] // 2
    left = [shift(rows, "z", step) for step in (1, 2)]
    right = [shift(rows, "z", -step) for step in (1, 2)]
    left.append(shift(left[1], "z", 1))
    right.append(shift(right[1], "z", -1))
    first = shift(left[1][:half], "z", 2)
    second = shift(right[1][half:], "z", -2)
    return [rows, *left, *right, first, second]


def to_groups(slots):
    return [slots[0]] + [shift(slots[d], "head", d) for d in range(1, GROUPS)]


def from_groups(slots):
    return [slots[0]] + [shift(slots[d], "head", -d) for d in range(1, GROUPS)]


def on_device(
    image_input_rows,
    adapter_down_weight,
    adapter_up_weight,
    image_query_rows,
    image_key_rows,
    image_value_codes,
    value_fraction,
    value_step_sizes,
    timestep_group,
    timestep,
    image_output_grad,
    text_query_rows,
    text_key_rows,
    text_value_rows,
    text_output_grad,
):
    x_index, z_index = lax.axis_index("x"), lax.axis_index("z")
    core_index, group_index = lax.axis_index("core"), lax.axis_index("head")
    place = jnp.stack([x_index, z_index, core_index, group_index]).astype(jnp.int32)

    slots = pack_rows(place, image_query_rows, image_output_grad, image_key_rows, image_value_codes)
    slots = to_groups(slots)
    own, key_flat = join_slots(slots)
    gk = lax.all_gather(key_flat, ("x", "core"), axis=0, tiled=True)
    gk = gk.reshape(8 * GROUPS, 2, TOKENS, WIDTH)

    pieces = ring_pieces(own)
    stats, qa, ga, ka, va = row_stats(
        place,
        timestep_group,
        timestep,
        value_step_sizes,
        pieces,
        gk,
        text_query_rows,
        text_output_grad,
        text_key_rows,
        text_value_rows,
    )

    input_rows, up_weight, stats = lax.optimization_barrier(
        (image_input_rows, adapter_up_weight, stats)
    )
    stats = lax.all_to_all(stats, "z", split_axis=0, concat_axis=0, tiled=True)
    more = to_groups(pack_more(place, input_rows, value_fraction, adapter_down_weight.T))
    more = jnp.concatenate(more, axis=0)
    up_own = lax.dynamic_slice_in_dim(up_weight, group_index * WIDTH, WIDTH, 1)

    dq_part, keep_v, send_v, keep_k, send_k = row_grads(place, qa, ga, ka, va, stats)
    dq_own = lax.psum_scatter(
        dq_part.reshape(8 * (OWN + 16), WIDTH), "z", scatter_dimension=0, tiled=True
    )

    sum_v = keep_v + flip(send_v, "core", 1).astype(F32)
    low_v = sum_v.astype(BF16)
    arrived_v = [shift(low_v[d], "x", d) for d in range(1, 4)]
    dv_slots, low_part, up_part, steps_part = value_terms(
        sum_v[0], *arrived_v, key_flat, more, up_own
    )
    low_parts = [low_part] + [shift(low_part, "head", d) for d in range(1, GROUPS)]
    keep_a, send_a = adapter_terms(place, *low_parts, more, up_part, steps_part)
    sum_a = keep_a + flip(send_a, "core", 1)
    low_a = sum_a.astype(BF16)
    total = sum_a[0]
    for d in range(1, 4):
        total = total + shift(low_a[d], "x", d).astype(F32)

    sum_k = keep_k + flip(send_k, "core", 1).astype(F32)
    low_k = sum_k.astype(BF16)
    total_k = sum_k[0]
    for d in range(1, 4):
        total_k = total_k + shift(low_k[d], "x", d).astype(F32)
    total_k = total_k.astype(BF16)

    total, dq_own = lax.optimization_barrier((total, dq_own))
    for bit in (1, 2, 4):
        rounded = total.astype(BF16)
        total = rounded.astype(F32) + flip(rounded, "z", bit).astype(F32)
    total, total_k = lax.optimization_barrier((total.astype(BF16), total_k))
    by_x = jnp.stack([total] + [shift(total, "x", d) for d in range(1, 4)])
    back = jnp.stack(
        [
            dq_own[:OWN].reshape(GROUPS, TOKENS, WIDTH),
            total_k[:OWN].reshape(GROUPS, TOKENS, WIDTH),
            dv_slots,
        ],
        axis=1,
    )
    by_x, returned = lax.optimization_barrier((by_x, from_groups(back)))
    dq_img, dk_img, image_value_grad, dq_txt, dk_txt, dv_txt = place_rows(
        place, returned, image_value_codes, dq_own, total_k
    )
    by_group = jnp.stack([by_x] + [shift(by_x, "head", d) for d in range(1, GROUPS)])
    other = flip(by_group, "core", 1)
    grad_down, grad_up, grad_steps = place_totals(
        place, timestep_group, timestep, by_group, other
    )
    return (
        dq_img,
        dk_img,
        image_value_grad,
        dq_txt,
        dk_txt,
        dv_txt,
        grad_down.T,
        grad_up,
        grad_steps,
    )


def solution(mesh):
    fine = Mesh(mesh.devices.reshape(4, 8, 2, 4), ("x", "z", "core", "head"))
    seq = ("x", "z", "core")
    tokens = P(seq + ("head",), None)
    heads = P(None, "head")
    return jax.shard_map(
        on_device,
        mesh=fine,
        in_specs=(
            tokens,
            P(),
            P(),
            tokens,
            tokens,
            tokens,
            tokens,
            P(),
            P(),
            P(),
            tokens,
            heads,
            heads,
            heads,
            heads,
        ),
        out_specs=(
            tokens,
            tokens,
            tokens,
            P(seq, "head"),
            P(seq, "head"),
            P(seq, "head"),
            P(),
            P(),
            P(),
        ),
        check_vma=False,
    )
```

```python
import functools
import math

import jax
import jax.numpy as jnp
from jax import lax
from jax.experimental import pallas as pl
from jax.experimental.pallas import tpu as pltpu
from jax.sharding import Mesh
from jax.sharding import PartitionSpec as P

HEAD_SIZE = 128
QMAX = 127
UNSCALE = 0.0078125
SCALE = HEAD_SIZE ** -0.5
SCALE_LOG2 = SCALE * math.log2(math.e)

OWN = 128
IMG_ROWS = 1024
TXT_ROWS = 64
ROWS = IMG_ROWS + TXT_ROWS
HEADS = 3
WIDTH = HEADS * HEAD_SIZE
TOKENS = 32
GROUPS = 4
RANK = 64
DOWN = 768
LANES = 1280
LINE = 1152
CHUNK = OWN + 16
CUT = 80
TILE = 512

BF16 = jnp.bfloat16
F32 = jnp.float32
NT = (((1,), (1,)), ((), ()))
NN = (((1,), (0,)), ((), ()))
TN = (((0,), (0,)), ((), ()))


def dot(a, b, dims):
    return lax.dot_general(a, b, dims, preferred_element_type=F32)


def shift(rows, axis, step):
    size = lax.axis_size(axis)
    return lax.ppermute(rows, axis, [(i, (i + step) % size) for i in range(size)])


def flip(rows, axis, bit):
    size = lax.axis_size(axis)
    return lax.ppermute(rows, axis, [(i, i ^ bit) for i in range(size)])


def smem():
    return pl.BlockSpec(memory_space=pltpu.SMEM)


def vmem():
    return pl.BlockSpec(memory_space=pltpu.VMEM)


def params():
    return pltpu.CompilerParams(vmem_limit_bytes=56 << 20)


def shape(dims, dtype=BF16):
    return jax.ShapeDtypeStruct(dims, dtype)


def wrap(index, size):
    return lax.rem(index, size)


def columns(group, width):
    return pl.ds(pl.multiple_of(group * width, HEAD_SIZE), width)


def pack_kernel(place, q, g, k, codes, *outs):
    y = place[3]
    for d in range(GROUPS):
        at = columns(wrap(y + d, GROUPS), WIDTH)
        outs[d][0] = q[:, at]
        outs[d][1] = g[:, at]
        outs[d][2] = k[:, at]
        outs[d][3] = codes[:, at].astype(F32).astype(BF16)


def pack_rows(place, *rows):
    return pl.pallas_call(
        pack_kernel,
        in_specs=[smem()] + [vmem()] * 4,
        out_specs=[vmem()] * GROUPS,
        out_shape=[shape((4, TOKENS, WIDTH))] * GROUPS,
        name="pack_rows",
        compiler_params=params(),
    )(place, *rows)


def join_kernel(s0, s1, s2, s3, rows, keys):
    for d, slot in enumerate((s0, s1, s2, s3)):
        rows[d * TOKENS:(d + 1) * TOKENS] = slot[0]
        rows[OWN + d * TOKENS:OWN + (d + 1) * TOKENS] = slot[1]
        keys[2 * d * TOKENS:(2 * d + 1) * TOKENS] = slot[2]
        keys[(2 * d + 1) * TOKENS:(2 * d + 2) * TOKENS] = slot[3]


def join_slots(slots):
    return pl.pallas_call(
        join_kernel,
        in_specs=[vmem()] * GROUPS,
        out_specs=[vmem()] * 2,
        out_shape=[shape((2 * OWN, WIDTH))] * 2,
        name="join_slots",
        compiler_params=params(),
    )(*slots)


def pack_more_kernel(place, x, fraction, down_t, *outs):
    y = place[3]
    low = dot(x[...], down_t[...], NT).astype(BF16)
    blank = jnp.zeros((TOKENS, HEAD_SIZE - RANK), BF16)
    for d in range(GROUPS):
        group = wrap(y + d, GROUPS)
        outs[d][:, 0:DOWN] = x[:, columns(group, DOWN)]
        outs[d][:, DOWN:DOWN + WIDTH] = fraction[:, columns(group, WIDTH)]
        outs[d][:, DOWN + WIDTH:LANES] = jnp.concatenate([low, blank], axis=1)


def pack_more(place, *rows):
    return pl.pallas_call(
        pack_more_kernel,
        in_specs=[smem()] + [vmem()] * 3,
        out_specs=[vmem()] * GROUPS,
        out_shape=[shape((TOKENS, LANES))] * GROUPS,
        name="pack_more",
        compiler_params=params(),
    )(place, *rows)


def query_tiles():
    return [(s, TILE) for s in range(0, IMG_ROWS, TILE)] + [(IMG_ROWS, TXT_ROWS)]


PIECES = 9


def place_pieces(qa, ga, pieces, z):
    for piece, step in zip(pieces[:7], (0, 7, 6, 5, 1, 2, 3)):
        start = pl.multiple_of(wrap(z + step, 8) * OWN, OWN)
        qa[pl.ds(start, OWN)] = piece[0:OWN]
        ga[pl.ds(start, OWN)] = piece[OWN:2 * OWN]
    start = pl.multiple_of(wrap(z + 4, 8) * OWN, OWN)
    qa[pl.ds(start, OWN)] = pieces[7][...]
    ga[pl.ds(start, OWN)] = pieces[8][...]


def query_text(text, place):
    row = lax.broadcasted_iota(jnp.int32, (TXT_ROWS, 512), 0)
    column = lax.broadcasted_iota(jnp.int32, (TXT_ROWS, 512), 1)
    wanted = lax.shift_right_logical(row, 3) * 16 + lax.bitwise_and(row, 7)
    pick = jnp.where(column == wanted + place[0] * 128 + place[2] * 8, 1.0, 0.0).astype(BF16)
    return dot(pick, text[...], NN).astype(BF16)


def key_text(text, place):
    row = lax.broadcasted_iota(jnp.int32, (TXT_ROWS, 512), 0)
    column = lax.broadcasted_iota(jnp.int32, (TXT_ROWS, 512), 1)
    block = lax.shift_right_logical(row, 4) * 128 + lax.bitwise_and(row, 15)
    pick = jnp.where(column == block + place[1] * 16, 1.0, 0.0).astype(BF16)
    return dot(pick, text[...], NN).astype(BF16)


def rows_spec(rows):
    return pl.BlockSpec((rows, HEAD_SIZE), lambda h: (0, h))


def line_spec(copies):
    return pl.BlockSpec((copies, 2, LINE), lambda h: (0, 0, h))


def cost(matmuls, moved):
    return pl.CostEstimate(
        flops=2 * matmuls * HEADS * ROWS * ROWS * HEAD_SIZE,
        bytes_accessed=moved << 20,
        transcendentals=HEADS * ROWS * ROWS,
    )


def chunk_spec(rows):
    return pl.BlockSpec((4, rows, HEAD_SIZE), lambda h: (0, 0, h))


def stat_kernel(place, group, timestep, sizes, *refs):
    pieces = refs[:PIECES]
    mine, other, qt, gt, kt, vt, out, qa, ga, ka, va = refs[PIECES:]
    x, c = place[0], place[2]
    step = sizes[group[timestep[0]], place[3] * HEADS + pl.program_id(0)]
    place_pieces(qa, ga, pieces, place[1])
    qa[IMG_ROWS:ROWS] = query_text(qt, place)
    ga[IMG_ROWS:ROWS] = query_text(gt, place)
    ka[IMG_ROWS:ROWS] = key_text(kt, place)
    va[IMG_ROWS:ROWS] = key_text(vt, place)
    for i, e in enumerate((0, 3, 1, 2)):
        for core, part in ((c, mine), (1 - c, other)):
            start = pl.multiple_of((wrap(x + e, 4) * 2 + core) * OWN, OWN)
            pairs = part[i * 2 * OWN:(i + 1) * 2 * OWN].reshape(GROUPS, 2, TOKENS, HEAD_SIZE)
            ka[pl.ds(start, OWN)] = pairs[:, 0].reshape(OWN, HEAD_SIZE)
            codes = pairs[:, 1].reshape(OWN, HEAD_SIZE).astype(F32)
            va[pl.ds(start, OWN)] = (codes * step).astype(BF16)
    for s, n in query_tiles():
        st = dot(ka[...], qa[s:s + n], NT)
        m = jnp.max(st, axis=0, keepdims=True)
        e = jnp.exp2((st - m) * SCALE_LOG2)
        l = jnp.sum(e, axis=0, keepdims=True)
        dp = dot(va[...], ga[s:s + n], NT)
        w = jnp.sum(e * dp, axis=0, keepdims=True)
        lines = jnp.concatenate([m * SCALE_LOG2 + jnp.log2(l), w / l], axis=0)
        out[:, :, s:s + n] = jnp.broadcast_to(lines[None], (8, 2, n))
    out[:, :, ROWS:LINE] = jnp.zeros((8, 2, LINE - ROWS), F32)


def row_stats(place, group, timestep, sizes, pieces, *operands):
    return pl.pallas_call(
        stat_kernel,
        grid=(HEADS,),
        in_specs=[smem()] * 4
        + [rows_spec(2 * OWN)] * 7
        + [rows_spec(OWN)] * 2
        + [rows_spec(8 * OWN)] * 2
        + [rows_spec(512)] * 4,
        out_specs=[line_spec(8)] + [rows_spec(ROWS)] * 4,
        out_shape=[shape((8, 2, HEADS * LINE), F32)] + [shape((ROWS, WIDTH))] * 4,
        name="row_stats",
        compiler_params=params(),
        cost_estimate=cost(2, 8),
    )(place, group, timestep, sizes, *pieces, *operands)


def grad_kernel(place, qa, ga, ka, va, stats, *refs):
    outs, (keep, send, p_s, d_s, v_s, k_s, q_s) = refs[:7], refs[7:]
    x, z, c = place[0], place[1], place[2]
    logs, parts = stats[:, 0], stats[:, 1]
    m = jnp.max(logs, axis=0, keepdims=True)
    e = jnp.exp2(logs - m)
    l = jnp.sum(e, axis=0, keepdims=True)
    log = m + jnp.log2(l)
    delta = jnp.sum(e * parts, axis=0, keepdims=True) / l
    for s, n in query_tiles():
        st = dot(ka[...], qa[s:s + n], NT)
        p = jnp.exp2(st * SCALE_LOG2 - log[:, s:s + n])
        dp = dot(va[...], ga[s:s + n], NT)
        p_s[:, s:s + n] = p.astype(BF16)
        d_s[:, s:s + n] = (p * (dp - delta[:, s:s + n])).astype(BF16)
    v_s[...] = dot(p_s[...], ga[...], NN)
    k_s[...] = dot(d_s[...], qa[...], NN) * SCALE
    q_s[...] = dot(d_s[...], ka[...], TN) * SCALE
    blank = jnp.zeros((8, HEAD_SIZE), F32)
    own, two_up, two_down, near_up, near_down, half_up, half_down = outs
    for to, first, step in (
        (own, 0, 0),
        (two_up, 0, 2),
        (two_down, 0, 6),
        (near_up, 0, 3),
        (near_up, CHUNK, 1),
        (near_down, 0, 5),
        (near_down, CHUNK, 7),
    ):
        chunk = wrap(z + step, 8)
        rows = pl.ds(pl.multiple_of(chunk * OWN, OWN), OWN)
        text = pl.ds(pl.multiple_of(IMG_ROWS + chunk * 8, 8), 8)
        to[first:first + OWN] = q_s[rows].astype(to.dtype)
        tail = jnp.concatenate([q_s[text], blank], axis=0)
        to[first + OWN:first + CHUNK] = tail.astype(to.dtype)
    chunk = wrap(z + 4, 8)
    start = pl.multiple_of(chunk * OWN, OWN)
    text = pl.ds(pl.multiple_of(IMG_ROWS + chunk * 8, 8), 8)
    half_down[...] = q_s[pl.ds(start, CUT)].astype(BF16)
    half_up[0:OWN - CUT] = q_s[pl.ds(start + CUT, OWN - CUT)].astype(BF16)
    tail = jnp.concatenate([q_s[text], blank], axis=0)
    half_up[OWN - CUT:CHUNK - CUT] = tail.astype(BF16)
    for d in range(4):
        for core, to in ((c, keep), (1 - c, send)):
            chunk = wrap(x + d, 4) * 2 + core
            rows = pl.ds(pl.multiple_of(chunk * OWN, OWN), OWN)
            text = pl.ds(pl.multiple_of(IMG_ROWS + chunk * 8, 8), 8)
            to[d, 0:OWN] = v_s[rows].astype(to.dtype)
            to[d, OWN:2 * OWN] = k_s[rows].astype(to.dtype)
            both = jnp.concatenate([k_s[text], v_s[text]], axis=0)
            to[d, 2 * OWN:OWN + CHUNK] = both.astype(to.dtype)


def row_grads(place, *operands):
    return pl.pallas_call(
        grad_kernel,
        grid=(HEADS,),
        in_specs=[smem()] + [rows_spec(ROWS)] * 4 + [line_spec(8)],
        out_specs=[rows_spec(CHUNK)] * 3
        + [rows_spec(2 * CHUNK)] * 2
        + [rows_spec(CHUNK - CUT), rows_spec(CUT)]
        + [chunk_spec(OWN + CHUNK)] * 2,
        out_shape=[shape((CHUNK, WIDTH), F32)] * 3
        + [shape((2 * CHUNK, WIDTH))] * 2
        + [shape((CHUNK - CUT, WIDTH)), shape((CUT, WIDTH))]
        + [
            shape((4, OWN + CHUNK, WIDTH), F32),
            shape((4, OWN + CHUNK, WIDTH)),
        ],
        scratch_shapes=[pltpu.VMEM((ROWS, ROWS), BF16)] * 2
        + [pltpu.VMEM((ROWS, HEAD_SIZE), F32)] * 3,
        name="row_grads",
        compiler_params=params(),
        cost_estimate=cost(5, 12),
    )(place, *operands)


def value_kernel(own, r1, r2, r3, codes, m0, m1, m2, m3, up, dv, low, up_part, steps):
    total = own[0:OWN]
    for part in (r1, r2, r3):
        total = total + part[0:OWN].astype(F32)
    dv_quant = total.astype(BF16)
    dv[...] = dv_quant.reshape(GROUPS, TOKENS, WIDTH)
    pairs = codes[...].reshape(GROUPS, 2, TOKENS, WIDTH)
    code = pairs[:, 1].reshape(OWN, WIDTH).astype(F32)
    inside = jnp.abs(code) < QMAX
    rounded = dv_quant.astype(F32)
    image_grad = jnp.where(inside, rounded, 0.0).astype(BF16)
    low[...] = dot(image_grad, up[...], NT).astype(BF16)
    more = (m0, m1, m2, m3)
    low_input = jnp.concatenate([m[:, DOWN + WIDTH:DOWN + WIDTH + RANK] for m in more], axis=0)
    fraction = jnp.concatenate([m[:, DOWN:DOWN + WIDTH] for m in more], axis=0).astype(F32)
    up_part[...] = dot(low_input, image_grad, TN)
    terms = rounded * jnp.where(inside, -fraction, code)
    sums = jnp.sum(terms, axis=0, keepdims=True)
    lane = lax.broadcasted_iota(jnp.int32, (8, HEAD_SIZE), 1)
    row = lax.broadcasted_iota(jnp.int32, (8, HEAD_SIZE), 0)
    found = jnp.zeros((8, HEAD_SIZE), F32)
    for h in range(HEADS):
        head_sum = jnp.sum(sums[:, h * HEAD_SIZE:(h + 1) * HEAD_SIZE], axis=1, keepdims=True)
        found = found + jnp.where((lane == h) & (row == 0), head_sum, 0.0)
    steps[...] = found


def value_terms(*operands):
    return pl.pallas_call(
        value_kernel,
        in_specs=[vmem()] * 10,
        out_specs=[vmem()] * 4,
        out_shape=[
            shape((GROUPS, TOKENS, WIDTH)),
            shape((OWN, RANK)),
            shape((RANK, WIDTH), F32),
            shape((8, HEAD_SIZE), F32),
        ],
        name="value_terms",
        compiler_params=params(),
    )(*operands)


def adapter_kernel(place, low0, low1, low2, low3, m0, m1, m2, m3, up_part, steps, keep, send, whole):
    x, c = place[0], place[2]
    total = low0[...].astype(F32)
    for d, part in ((1, low1), (2, low2), (3, low3)):
        cut = (GROUPS - d) * TOKENS
        total = total + jnp.concatenate([part[cut:], part[:cut]], axis=0).astype(F32)
    x_rows = jnp.concatenate([m[:, 0:DOWN] for m in (m0, m1, m2, m3)], axis=0)
    whole[:, 0:DOWN] = dot(total.astype(BF16), x_rows, TN)
    whole[:, DOWN:DOWN + WIDTH] = up_part[...]
    whole[:, DOWN + WIDTH:LANES] = jnp.zeros((RANK, HEAD_SIZE), F32)
    whole[0:8, DOWN + WIDTH:LANES] = steps[...]
    for d in range(4):
        for core, to in ((c, keep), (1 - c, send)):
            start = (core * 4 + wrap(x + d, 4)) * 8
            to[d] = whole[pl.ds(pl.multiple_of(start, 8), 8)].astype(to.dtype)


def adapter_terms(place, *operands):
    return pl.pallas_call(
        adapter_kernel,
        in_specs=[smem()] + [vmem()] * 10,
        out_specs=[vmem()] * 2,
        out_shape=[shape((4, 8, LANES), F32), shape((4, 8, LANES), F32)],
        scratch_shapes=[pltpu.VMEM((RANK, LANES), F32)],
        name="adapter_terms",
        compiler_params=params(),
    )(place, *operands)


def place_kernel(place, group_table, timestep, mine, other, down_t, up, steps):
    x, c, y = place[0], place[2], place[3]
    slot_row = lax.broadcasted_iota(jnp.int32, (8, HEAD_SIZE), 0) == group_table[timestep[0]]
    lane = lax.broadcasted_iota(jnp.int32, (8, HEAD_SIZE), 1)
    row = lax.broadcasted_iota(jnp.int32, (8, HEAD_SIZE), 0)
    found = jnp.zeros((1, HEAD_SIZE), F32)
    for e in range(GROUPS):
        group = wrap(y + GROUPS - e, GROUPS)
        for core, part in ((c, mine), (1 - c, other)):
            for d in range(4):
                index = core * 4 + wrap(x + 4 - d, 4)
                rows = pl.ds(pl.multiple_of(index * 8, 8), 8)
                tile = part[e, d].astype(F32) * UNSCALE
                down_t[rows, columns(group, DOWN)] = tile[:, 0:DOWN]
                up[rows, columns(group, WIDTH)] = tile[:, DOWN:DOWN + WIDTH]
                last = tile[:, DOWN + WIDTH:LANES]
                for h in range(HEADS):
                    value = jnp.sum(jnp.where((lane == h) & (row == 0), last, 0.0), axis=0, keepdims=True)
                    value = jnp.sum(value, axis=1, keepdims=True)
                    hit = (lane[0:1] == group * HEADS + h) & (index == 0)
                    found = found + jnp.where(hit, value, 0.0)
    steps[...] = jnp.where(slot_row, found * QMAX ** -0.5, 0.0)[:, 0:GROUPS * HEADS]


def place_totals(place, group_table, timestep, mine, other):
    return pl.pallas_call(
        place_kernel,
        in_specs=[smem()] * 3 + [vmem()] * 2,
        out_specs=[vmem()] * 3,
        out_shape=[
            shape((RANK, GROUPS * DOWN), F32),
            shape((RANK, GROUPS * WIDTH), F32),
            shape((8, GROUPS * HEADS), F32),
        ],
        name="place_totals",
        compiler_params=params(),
    )(place, group_table, timestep, mine, other)


def place_rows_kernel(place, *refs):
    pieces, (codes, q_tail, k_tail, dq, dk, dv, q_txt, k_txt, v_txt) = refs[:GROUPS], refs[GROUPS:]
    y = place[3]
    q_txt[...] = q_tail[OWN:OWN + 16].astype(F32)[0:8].astype(BF16)
    tail = k_tail[OWN:OWN + 16].astype(F32)
    k_txt[...] = tail[0:8].astype(BF16)
    v_txt[...] = tail[8:16].astype(BF16)
    for d in range(GROUPS):
        at = columns(wrap(y + d, GROUPS), WIDTH)
        dq[:, at] = pieces[d][0]
        dk[:, at] = pieces[d][1]
        inside = jnp.abs(codes[:, at]) < QMAX
        value = pieces[d][2].astype(F32)
        dv[:, at] = jnp.where(inside, value, 0.0).astype(BF16)


def place_rows(place, pieces, codes, q_tail, k_tail):
    return pl.pallas_call(
        place_rows_kernel,
        in_specs=[smem()] + [vmem()] * (GROUPS + 3),
        out_specs=[vmem()] * 6,
        out_shape=[shape((TOKENS, GROUPS * WIDTH))] * 3 + [shape((8, WIDTH))] * 3,
        name="place_rows",
        compiler_params=params(),
    )(place, *pieces, codes, q_tail, k_tail)


def gather_rows(rows, keys):
    half = rows.shape[0] // 2
    up = [shift(rows, "z", step) for step in (2, 1)]
    down = [shift(rows, "z", -step) for step in (2, 1)]
    left, right = shift(keys, "x", 1), shift(keys, "x", -1)
    first, second = shift(left[:half], "x", 1), shift(right[half:], "x", -1)
    up, down, left, right, first, second = lax.optimization_barrier(
        (up, down, left, right, first, second)
    )
    up3, down3 = shift(up[0], "z", 1), shift(down[0], "z", -1)
    up4, down4 = shift(up[0][:half], "z", 2), shift(down[0][half:], "z", -2)
    mine = jnp.concatenate([keys, left, right, first, second], axis=0)
    pieces = [rows, up[1], up[0], up3, down[1], down[0], down3, up4, down4]
    return pieces, mine, flip(mine, "core", 1)


def to_groups(slots):
    return [slots[0]] + [shift(slots[d], "head", d) for d in range(1, GROUPS)]


def from_groups(slots):
    return [slots[0]] + [shift(slots[d], "head", -d) for d in range(1, GROUPS)]


def on_device(
    image_input_rows,
    adapter_down_weight,
    adapter_up_weight,
    image_query_rows,
    image_key_rows,
    image_value_codes,
    value_fraction,
    value_step_sizes,
    timestep_group,
    timestep,
    image_output_grad,
    text_query_rows,
    text_key_rows,
    text_value_rows,
    text_output_grad,
):
    x_index, z_index = lax.axis_index("x"), lax.axis_index("z")
    core_index, group_index = lax.axis_index("core"), lax.axis_index("head")
    place = jnp.stack([x_index, z_index, core_index, group_index]).astype(jnp.int32)

    slots = pack_rows(place, image_query_rows, image_output_grad, image_key_rows, image_value_codes)
    slots = to_groups(slots)
    own, key_flat = join_slots(slots)
    pieces, mine, other = gather_rows(own, key_flat)
    stats, qa, ga, ka, va = row_stats(
        place,
        timestep_group,
        timestep,
        value_step_sizes,
        pieces,
        mine,
        other,
        text_query_rows,
        text_output_grad,
        text_key_rows,
        text_value_rows,
    )

    input_rows, up_weight, stats = lax.optimization_barrier(
        (image_input_rows, adapter_up_weight, stats)
    )
    stats = lax.all_to_all(stats, "z", split_axis=0, concat_axis=0, tiled=True)
    more = to_groups(pack_more(place, input_rows, value_fraction, adapter_down_weight.T))
    stats, more = lax.optimization_barrier((stats, more))
    up_own = lax.dynamic_slice_in_dim(up_weight, group_index * WIDTH, WIDTH, 1)

    own_q, two_up, two_down, near_up, near_down, half_up, half_down, keep, send = row_grads(
        place, qa, ga, ka, va, stats
    )
    sums = keep + flip(send, "core", 1).astype(F32)
    low_sums, near_up, near_down = lax.optimization_barrier(
        (sums.astype(BF16), near_up, near_down)
    )

    arrived = [shift(low_sums[d], "x", d) for d in range(1, 4)]
    from_below = shift(near_up, "z", 1)
    from_above = shift(near_down, "z", -1)
    arrived, from_below, from_above = lax.optimization_barrier((arrived, from_below, from_above))
    dv_slots, low_part, up_part, steps_part = value_terms(
        sums[0], *arrived, key_flat, *more, up_own
    )
    low_part, half_up, half_down = lax.optimization_barrier((low_part, half_up, half_down))
    low_parts = [shift(low_part, "head", d) for d in range(1, GROUPS)]
    half_below = shift(half_up, "z", 2)
    half_above = shift(half_down, "z", -2)
    two_up = two_up + from_below[:CHUNK].astype(F32)
    two_up = two_up + jnp.pad(half_below.astype(F32), ((CUT, 0), (0, 0)))
    two_down = two_down + from_above[:CHUNK].astype(F32)
    two_down = two_down + jnp.pad(half_above.astype(F32), ((0, CHUNK - CUT), (0, 0)))
    dq_own = own_q + from_below[CHUNK:].astype(F32) + from_above[CHUNK:].astype(F32)

    two_up, two_down = two_up.astype(BF16), two_down.astype(BF16)
    keep_a, send_a = adapter_terms(place, low_part, *low_parts, *more, up_part, steps_part)
    total_k = sums[0, OWN:]
    for part in arrived:
        total_k = total_k + part[OWN:].astype(F32)
    total_k = total_k.astype(BF16)

    sum_a = keep_a + flip(send_a, "core", 1)
    low_a, two_up, two_down = lax.optimization_barrier((sum_a.astype(BF16), two_up, two_down))
    arrived_a = [shift(low_a[d], "x", d) for d in range(1, 4)]
    two_below = shift(two_up, "z", 2)
    two_above = shift(two_down, "z", -2)
    arrived_a, two_below, two_above = lax.optimization_barrier((arrived_a, two_below, two_above))
    total = sum_a[0]
    for part in arrived_a:
        total = total + part.astype(F32)
    dq_own = (dq_own + two_below.astype(F32) + two_above.astype(F32)).astype(BF16)
    back = jnp.stack(
        [
            dq_own[:OWN].reshape(GROUPS, TOKENS, WIDTH),
            total_k[:OWN].reshape(GROUPS, TOKENS, WIDTH),
            dv_slots,
        ],
        axis=1,
    )
    terms = jnp.broadcast_to(total.astype(BF16)[None], (8, 8, LANES))
    terms, back = lax.optimization_barrier((terms, back))
    terms = lax.all_to_all(terms, "z", split_axis=0, concat_axis=0, tiled=True)
    terms, returned = lax.optimization_barrier((terms, from_groups(back)))
    total = jnp.sum(terms.astype(F32), axis=0).astype(BF16)
    dq_img, dk_img, image_value_grad, dq_txt, dk_txt, dv_txt = place_rows(
        place, returned, image_value_codes, dq_own, total_k
    )
    by_x = jnp.stack([total] + [shift(total, "x", d) for d in range(1, 4)])
    by_group = jnp.stack([by_x] + [shift(by_x, "head", d) for d in range(1, GROUPS)])
    other = flip(by_group, "core", 1)
    grad_down, grad_up, grad_steps = place_totals(
        place, timestep_group, timestep, by_group, other
    )
    return (
        dq_img,
        dk_img,
        image_value_grad,
        dq_txt,
        dk_txt,
        dv_txt,
        grad_down.T,
        grad_up,
        grad_steps,
    )


def solution(mesh):
    fine = Mesh(mesh.devices.reshape(4, 8, 2, 4), ("x", "z", "core", "head"))
    seq = ("x", "z", "core")
    tokens = P(seq + ("head",), None)
    heads = P(None, "head")
    return jax.shard_map(
        on_device,
        mesh=fine,
        in_specs=(
            tokens,
            P(),
            P(),
            tokens,
            tokens,
            tokens,
            tokens,
            P(),
            P(),
            P(),
            tokens,
            heads,
            heads,
            heads,
            heads,
        ),
        out_specs=(
            tokens,
            tokens,
            tokens,
            P(seq, "head"),
            P(seq, "head"),
            P(seq, "head"),
            P(),
            P(),
            P(),
        ),
        check_vma=False,
    )
```

```python
import functools
import math

import jax
import jax.numpy as jnp
from jax import lax
from jax.experimental import pallas as pl
from jax.experimental.pallas import tpu as pltpu
from jax.sharding import Mesh
from jax.sharding import PartitionSpec as P

HEAD_SIZE = 128
QMAX = 127
UNSCALE = 0.0078125
SCALE = HEAD_SIZE ** -0.5
SCALE_LOG2 = SCALE * math.log2(math.e)

OWN = 128
IMG_ROWS = 1024
TXT_ROWS = 64
ROWS = IMG_ROWS + TXT_ROWS
HEADS = 3
WIDTH = HEADS * HEAD_SIZE
TOKENS = 32
GROUPS = 4
RANK = 64
DOWN = 768
LANES = 1280
LINE = 1152
CHUNK = OWN + 16
TILE = 512

BF16 = jnp.bfloat16
F32 = jnp.float32
NT = (((1,), (1,)), ((), ()))
NN = (((1,), (0,)), ((), ()))
TN = (((0,), (0,)), ((), ()))


def dot(a, b, dims):
    return lax.dot_general(a, b, dims, preferred_element_type=F32)


def shift(rows, axis, step):
    size = lax.axis_size(axis)
    return lax.ppermute(rows, axis, [(i, (i + step) % size) for i in range(size)])


def flip(rows, axis, bit):
    size = lax.axis_size(axis)
    return lax.ppermute(rows, axis, [(i, i ^ bit) for i in range(size)])


def smem():
    return pl.BlockSpec(memory_space=pltpu.SMEM)


def vmem():
    return pl.BlockSpec(memory_space=pltpu.VMEM)


def params():
    return pltpu.CompilerParams(vmem_limit_bytes=56 << 20)


def shape(dims, dtype=BF16):
    return jax.ShapeDtypeStruct(dims, dtype)


def wrap(index, size):
    return lax.rem(index, size)


def columns(group, width):
    return pl.ds(pl.multiple_of(group * width, HEAD_SIZE), width)


def pack_kernel(place, q, g, k, codes, *outs):
    y = place[3]
    for d in range(GROUPS):
        at = columns(wrap(y + d, GROUPS), WIDTH)
        outs[d][0] = q[:, at]
        outs[d][1] = g[:, at]
        outs[d][2] = k[:, at]
        outs[d][3] = codes[:, at].astype(F32).astype(BF16)


def pack_rows(place, *rows):
    return pl.pallas_call(
        pack_kernel,
        in_specs=[smem()] + [vmem()] * 4,
        out_specs=[vmem()] * GROUPS,
        out_shape=[shape((4, TOKENS, WIDTH))] * GROUPS,
        name="pack_rows",
        compiler_params=params(),
    )(place, *rows)


def join_kernel(s0, s1, s2, s3, rows, keys):
    for d, slot in enumerate((s0, s1, s2, s3)):
        rows[d * TOKENS:(d + 1) * TOKENS] = slot[0]
        rows[OWN + d * TOKENS:OWN + (d + 1) * TOKENS] = slot[1]
        keys[2 * d * TOKENS:(2 * d + 1) * TOKENS] = slot[2]
        keys[(2 * d + 1) * TOKENS:(2 * d + 2) * TOKENS] = slot[3]


def join_slots(slots):
    return pl.pallas_call(
        join_kernel,
        in_specs=[vmem()] * GROUPS,
        out_specs=[vmem()] * 2,
        out_shape=[shape((2 * OWN, WIDTH))] * 2,
        name="join_slots",
        compiler_params=params(),
    )(*slots)


def pack_more_kernel(place, x, fraction, down_t, *outs):
    y = place[3]
    low = dot(x[...], down_t[...], NT).astype(BF16)
    blank = jnp.zeros((TOKENS, HEAD_SIZE - RANK), BF16)
    for d in range(GROUPS):
        group = wrap(y + d, GROUPS)
        outs[d][:, 0:DOWN] = x[:, columns(group, DOWN)]
        outs[d][:, DOWN:DOWN + WIDTH] = fraction[:, columns(group, WIDTH)]
        outs[d][:, DOWN + WIDTH:LANES] = jnp.concatenate([low, blank], axis=1)


def pack_more(place, *rows):
    return pl.pallas_call(
        pack_more_kernel,
        in_specs=[smem()] + [vmem()] * 3,
        out_specs=[vmem()] * GROUPS,
        out_shape=[shape((TOKENS, LANES))] * GROUPS,
        name="pack_more",
        compiler_params=params(),
    )(place, *rows)


def query_tiles():
    return [(s, TILE) for s in range(0, IMG_ROWS, TILE)] + [(IMG_ROWS, TXT_ROWS)]


PIECES = 9


def place_pieces(qa, ga, pieces, z):
    for piece, step in zip(pieces[:7], (0, 7, 6, 5, 1, 2, 3)):
        start = pl.multiple_of(wrap(z + step, 8) * OWN, OWN)
        qa[pl.ds(start, OWN)] = piece[0:OWN]
        ga[pl.ds(start, OWN)] = piece[OWN:2 * OWN]
    start = pl.multiple_of(wrap(z + 4, 8) * OWN, OWN)
    qa[pl.ds(start, OWN)] = pieces[7][...]
    ga[pl.ds(start, OWN)] = pieces[8][...]


def query_text(text, place):
    row = lax.broadcasted_iota(jnp.int32, (TXT_ROWS, 512), 0)
    column = lax.broadcasted_iota(jnp.int32, (TXT_ROWS, 512), 1)
    wanted = lax.shift_right_logical(row, 3) * 16 + lax.bitwise_and(row, 7)
    pick = jnp.where(column == wanted + place[0] * 128 + place[2] * 8, 1.0, 0.0).astype(BF16)
    return dot(pick, text[...], NN).astype(BF16)


def key_text(text, place):
    row = lax.broadcasted_iota(jnp.int32, (TXT_ROWS, 512), 0)
    column = lax.broadcasted_iota(jnp.int32, (TXT_ROWS, 512), 1)
    block = lax.shift_right_logical(row, 4) * 128 + lax.bitwise_and(row, 15)
    pick = jnp.where(column == block + place[1] * 16, 1.0, 0.0).astype(BF16)
    return dot(pick, text[...], NN).astype(BF16)


def rows_spec(rows):
    return pl.BlockSpec((rows, HEAD_SIZE), lambda h: (0, h))


def line_spec(copies):
    return pl.BlockSpec((copies, 2, LINE), lambda h: (0, 0, h))


def cost(matmuls, moved):
    return pl.CostEstimate(
        flops=2 * matmuls * HEADS * ROWS * ROWS * HEAD_SIZE,
        bytes_accessed=moved << 20,
        transcendentals=HEADS * ROWS * ROWS,
    )


def chunk_spec(rows):
    return pl.BlockSpec((4, rows, HEAD_SIZE), lambda h: (0, 0, h))


def stat_kernel(place, group, timestep, sizes, *refs):
    pieces = refs[:PIECES]
    mine, other, qt, gt, kt, vt, out, qa, ga, ka, va = refs[PIECES:]
    x, c = place[0], place[2]
    step = sizes[group[timestep[0]], place[3] * HEADS + pl.program_id(0)]
    place_pieces(qa, ga, pieces, place[1])
    qa[IMG_ROWS:ROWS] = query_text(qt, place)
    ga[IMG_ROWS:ROWS] = query_text(gt, place)
    ka[IMG_ROWS:ROWS] = key_text(kt, place)
    va[IMG_ROWS:ROWS] = key_text(vt, place)
    for i, e in enumerate((0, 3, 1, 2)):
        for core, part in ((c, mine), (1 - c, other)):
            start = pl.multiple_of((wrap(x + e, 4) * 2 + core) * OWN, OWN)
            pairs = part[i * 2 * OWN:(i + 1) * 2 * OWN].reshape(GROUPS, 2, TOKENS, HEAD_SIZE)
            ka[pl.ds(start, OWN)] = pairs[:, 0].reshape(OWN, HEAD_SIZE)
            codes = pairs[:, 1].reshape(OWN, HEAD_SIZE).astype(F32)
            va[pl.ds(start, OWN)] = (codes * step).astype(BF16)
    for s, n in query_tiles():
        st = dot(ka[...], qa[s:s + n], NT)
        m = jnp.max(st, axis=0, keepdims=True)
        e = jnp.exp2((st - m) * SCALE_LOG2)
        l = jnp.sum(e, axis=0, keepdims=True)
        dp = dot(va[...], ga[s:s + n], NT)
        w = jnp.sum(e * dp, axis=0, keepdims=True)
        lines = jnp.concatenate([m * SCALE_LOG2 + jnp.log2(l), w / l], axis=0)
        out[:, :, s:s + n] = jnp.broadcast_to(lines[None], (8, 2, n))
    out[:, :, ROWS:LINE] = jnp.zeros((8, 2, LINE - ROWS), F32)


def row_stats(place, group, timestep, sizes, pieces, *operands):
    return pl.pallas_call(
        stat_kernel,
        grid=(HEADS,),
        in_specs=[smem()] * 4
        + [rows_spec(2 * OWN)] * 7
        + [rows_spec(OWN)] * 2
        + [rows_spec(8 * OWN)] * 2
        + [rows_spec(512)] * 4,
        out_specs=[line_spec(8)] + [rows_spec(ROWS)] * 4,
        out_shape=[shape((8, 2, HEADS * LINE), F32)] + [shape((ROWS, WIDTH))] * 4,
        name="row_stats",
        compiler_params=params(),
        cost_estimate=cost(2, 8),
    )(place, group, timestep, sizes, *pieces, *operands)


def grad_kernel(place, qa, ga, ka, va, stats, *refs):
    outs, (keep_v, send_v, keep_k, send_k, p_s, d_s, v_s, k_s, q_s) = refs[:6], refs[6:]
    x, z, c = place[0], place[1], place[2]
    logs, parts = stats[:, 0], stats[:, 1]
    m = jnp.max(logs, axis=0, keepdims=True)
    e = jnp.exp2(logs - m)
    l = jnp.sum(e, axis=0, keepdims=True)
    log = m + jnp.log2(l)
    delta = jnp.sum(e * parts, axis=0, keepdims=True) / l
    for s, n in query_tiles():
        st = dot(ka[...], qa[s:s + n], NT)
        p = jnp.exp2(st * SCALE_LOG2 - log[:, s:s + n])
        dp = dot(va[...], ga[s:s + n], NT)
        p_s[:, s:s + n] = p.astype(BF16)
        d_s[:, s:s + n] = (p * (dp - delta[:, s:s + n])).astype(BF16)
    v_s[...] = dot(p_s[...], ga[...], NN)
    k_s[...] = dot(d_s[...], qa[...], NN) * SCALE
    q_s[...] = dot(d_s[...], ka[...], TN) * SCALE
    blank = jnp.zeros((8, HEAD_SIZE), F32)
    own, two_up, two_down, near_up, near_down, far = outs
    for to, first, step in (
        (own, 0, 0),
        (two_up, 0, 2),
        (two_down, 0, 6),
        (near_up, 0, 3),
        (near_up, CHUNK, 1),
        (near_down, 0, 5),
        (near_down, CHUNK, 7),
        (far, 0, 4),
    ):
        chunk = wrap(z + step, 8)
        rows = pl.ds(pl.multiple_of(chunk * OWN, OWN), OWN)
        text = pl.ds(pl.multiple_of(IMG_ROWS + chunk * 8, 8), 8)
        to[first:first + OWN] = q_s[rows].astype(to.dtype)
        tail = jnp.concatenate([q_s[text], blank], axis=0)
        to[first + OWN:first + CHUNK] = tail.astype(to.dtype)
    for d in range(4):
        for core, to_v, to_k in ((c, keep_v, keep_k), (1 - c, send_v, send_k)):
            chunk = wrap(x + d, 4) * 2 + core
            rows = pl.ds(pl.multiple_of(chunk * OWN, OWN), OWN)
            text = pl.ds(pl.multiple_of(IMG_ROWS + chunk * 8, 8), 8)
            to_v[d] = v_s[rows].astype(to_v.dtype)
            to_k[d, 0:OWN] = k_s[rows].astype(to_k.dtype)
            both = jnp.concatenate([k_s[text], v_s[text]], axis=0)
            to_k[d, OWN:CHUNK] = both.astype(to_k.dtype)


def row_grads(place, *operands):
    return pl.pallas_call(
        grad_kernel,
        grid=(HEADS,),
        in_specs=[smem()] + [rows_spec(ROWS)] * 4 + [line_spec(8)],
        out_specs=[rows_spec(CHUNK)] * 3
        + [rows_spec(2 * CHUNK)] * 2
        + [rows_spec(CHUNK)]
        + [chunk_spec(OWN)] * 2
        + [chunk_spec(CHUNK)] * 2,
        out_shape=[shape((CHUNK, WIDTH), F32)] * 3
        + [shape((2 * CHUNK, WIDTH))] * 2
        + [shape((CHUNK, WIDTH))]
        + [
            shape((4, OWN, WIDTH), F32),
            shape((4, OWN, WIDTH)),
            shape((4, CHUNK, WIDTH), F32),
            shape((4, CHUNK, WIDTH)),
        ],
        scratch_shapes=[pltpu.VMEM((ROWS, ROWS), BF16)] * 2
        + [pltpu.VMEM((ROWS, HEAD_SIZE), F32)] * 3,
        name="row_grads",
        compiler_params=params(),
        cost_estimate=cost(5, 12),
    )(place, *operands)


def value_kernel(place, own, r1, r2, r3, codes, m0, m1, m2, m3, up, dv, low, up_part, steps):
    total = own[...]
    for part in (r1, r2, r3):
        total = total + part[...].astype(F32)
    dv_quant = total.astype(BF16)
    dv[...] = dv_quant.reshape(GROUPS, TOKENS, WIDTH)
    pairs = codes[...].reshape(GROUPS, 2, TOKENS, WIDTH)
    code = pairs[:, 1].reshape(OWN, WIDTH).astype(F32)
    inside = jnp.abs(code) < QMAX
    rounded = dv_quant.astype(F32)
    image_grad = jnp.where(inside, rounded, 0.0).astype(BF16)
    up_own = up[:, columns(place[3], WIDTH)]
    low[...] = dot(image_grad, up_own, NT).astype(BF16)
    more = (m0, m1, m2, m3)
    low_input = jnp.concatenate([m[:, DOWN + WIDTH:DOWN + WIDTH + RANK] for m in more], axis=0)
    fraction = jnp.concatenate([m[:, DOWN:DOWN + WIDTH] for m in more], axis=0).astype(F32)
    up_part[...] = dot(low_input, image_grad, TN)
    terms = rounded * jnp.where(inside, -fraction, code)
    sums = jnp.sum(terms, axis=0, keepdims=True)
    lane = lax.broadcasted_iota(jnp.int32, (8, HEAD_SIZE), 1)
    row = lax.broadcasted_iota(jnp.int32, (8, HEAD_SIZE), 0)
    found = jnp.zeros((8, HEAD_SIZE), F32)
    for h in range(HEADS):
        head_sum = jnp.sum(sums[:, h * HEAD_SIZE:(h + 1) * HEAD_SIZE], axis=1, keepdims=True)
        found = found + jnp.where((lane == h) & (row == 0), head_sum, 0.0)
    steps[...] = found


def value_terms(place, *operands):
    return pl.pallas_call(
        value_kernel,
        in_specs=[smem()] + [vmem()] * 10,
        out_specs=[vmem()] * 4,
        out_shape=[
            shape((GROUPS, TOKENS, WIDTH)),
            shape((OWN, RANK)),
            shape((RANK, WIDTH), F32),
            shape((8, HEAD_SIZE), F32),
        ],
        name="value_terms",
        compiler_params=params(),
    )(place, *operands)


def adapter_kernel(place, low0, low1, low2, low3, m0, m1, m2, m3, up_part, steps, keep, send, whole):
    x, c = place[0], place[2]
    total = low0[...].astype(F32)
    for d, part in ((1, low1), (2, low2), (3, low3)):
        cut = (GROUPS - d) * TOKENS
        total = total + jnp.concatenate([part[cut:], part[:cut]], axis=0).astype(F32)
    x_rows = jnp.concatenate([m[:, 0:DOWN] for m in (m0, m1, m2, m3)], axis=0)
    whole[:, 0:DOWN] = dot(total.astype(BF16), x_rows, TN)
    whole[:, DOWN:DOWN + WIDTH] = up_part[...]
    whole[:, DOWN + WIDTH:LANES] = jnp.zeros((RANK, HEAD_SIZE), F32)
    whole[0:8, DOWN + WIDTH:LANES] = steps[...]
    for d in range(4):
        for core, to in ((c, keep), (1 - c, send)):
            start = (core * 4 + wrap(x + d, 4)) * 8
            to[d] = whole[pl.ds(pl.multiple_of(start, 8), 8)].astype(to.dtype)


def adapter_terms(place, *operands):
    return pl.pallas_call(
        adapter_kernel,
        in_specs=[smem()] + [vmem()] * 10,
        out_specs=[vmem()] * 2,
        out_shape=[shape((4, 8, LANES), F32), shape((4, 8, LANES), F32)],
        scratch_shapes=[pltpu.VMEM((RANK, LANES), F32)],
        name="adapter_terms",
        compiler_params=params(),
    )(place, *operands)


def place_kernel(place, group_table, timestep, mine, other, down_t, up, steps):
    x, c, y = place[0], place[2], place[3]
    slot_row = lax.broadcasted_iota(jnp.int32, (8, HEAD_SIZE), 0) == group_table[timestep[0]]
    lane = lax.broadcasted_iota(jnp.int32, (8, HEAD_SIZE), 1)
    row = lax.broadcasted_iota(jnp.int32, (8, HEAD_SIZE), 0)
    found = jnp.zeros((1, HEAD_SIZE), F32)
    for e in range(GROUPS):
        group = wrap(y + GROUPS - e, GROUPS)
        for core, part in ((c, mine), (1 - c, other)):
            for d in range(4):
                index = core * 4 + wrap(x + 4 - d, 4)
                rows = pl.ds(pl.multiple_of(index * 8, 8), 8)
                tile = part[e, d].astype(F32) * UNSCALE
                down_t[rows, columns(group, DOWN)] = tile[:, 0:DOWN]
                up[rows, columns(group, WIDTH)] = tile[:, DOWN:DOWN + WIDTH]
                last = tile[:, DOWN + WIDTH:LANES]
                for h in range(HEADS):
                    value = jnp.sum(jnp.where((lane == h) & (row == 0), last, 0.0), axis=0, keepdims=True)
                    value = jnp.sum(value, axis=1, keepdims=True)
                    hit = (lane[0:1] == group * HEADS + h) & (index == 0)
                    found = found + jnp.where(hit, value, 0.0)
    steps[...] = jnp.where(slot_row, found * QMAX ** -0.5, 0.0)[:, 0:GROUPS * HEADS]


def place_totals(place, group_table, timestep, mine, other):
    return pl.pallas_call(
        place_kernel,
        in_specs=[smem()] * 3 + [vmem()] * 2,
        out_specs=[vmem()] * 3,
        out_shape=[
            shape((RANK, GROUPS * DOWN), F32),
            shape((RANK, GROUPS * WIDTH), F32),
            shape((8, GROUPS * HEADS), F32),
        ],
        name="place_totals",
        compiler_params=params(),
    )(place, group_table, timestep, mine, other)


def place_rows_kernel(place, *refs):
    pieces, (codes, q_tail, k_tail, dq, dk, dv, q_txt, k_txt, v_txt) = refs[:GROUPS], refs[GROUPS:]
    y = place[3]
    q_txt[...] = q_tail[OWN:OWN + 16].astype(F32)[0:8].astype(BF16)
    tail = k_tail[OWN:OWN + 16].astype(F32)
    k_txt[...] = tail[0:8].astype(BF16)
    v_txt[...] = tail[8:16].astype(BF16)
    for d in range(GROUPS):
        at = columns(wrap(y + d, GROUPS), WIDTH)
        dq[:, at] = pieces[d][0]
        dk[:, at] = pieces[d][1]
        inside = jnp.abs(codes[:, at]) < QMAX
        value = pieces[d][2].astype(F32)
        dv[:, at] = jnp.where(inside, value, 0.0).astype(BF16)


def place_rows(place, pieces, codes, q_tail, k_tail):
    return pl.pallas_call(
        place_rows_kernel,
        in_specs=[smem()] + [vmem()] * (GROUPS + 3),
        out_specs=[vmem()] * 6,
        out_shape=[shape((TOKENS, GROUPS * WIDTH))] * 3 + [shape((8, WIDTH))] * 3,
        name="place_rows",
        compiler_params=params(),
    )(place, *pieces, codes, q_tail, k_tail)


def gather_rows(rows, keys):
    half = rows.shape[0] // 2
    up = [shift(rows, "z", step) for step in (2, 1)]
    down = [shift(rows, "z", -step) for step in (2, 1)]
    left, right = shift(keys, "x", 1), shift(keys, "x", -1)
    first, second = shift(left[:half], "x", 1), shift(right[half:], "x", -1)
    up, down, left, right, first, second = lax.optimization_barrier(
        (up, down, left, right, first, second)
    )
    up3, down3 = shift(up[0], "z", 1), shift(down[0], "z", -1)
    up4, down4 = shift(up[0][:half], "z", 2), shift(down[0][half:], "z", -2)
    mine = jnp.concatenate([keys, left, right, first, second], axis=0)
    pieces = [rows, up[1], up[0], up3, down[1], down[0], down3, up4, down4]
    return pieces, mine, flip(mine, "core", 1)


def to_groups(slots):
    return [slots[0]] + [shift(slots[d], "head", d) for d in range(1, GROUPS)]


def from_groups(slots):
    return [slots[0]] + [shift(slots[d], "head", -d) for d in range(1, GROUPS)]


def on_device(
    image_input_rows,
    adapter_down_weight,
    adapter_up_weight,
    image_query_rows,
    image_key_rows,
    image_value_codes,
    value_fraction,
    value_step_sizes,
    timestep_group,
    timestep,
    image_output_grad,
    text_query_rows,
    text_key_rows,
    text_value_rows,
    text_output_grad,
):
    x_index, z_index = lax.axis_index("x"), lax.axis_index("z")
    core_index, group_index = lax.axis_index("core"), lax.axis_index("head")
    place = jnp.stack([x_index, z_index, core_index, group_index]).astype(jnp.int32)

    slots = pack_rows(place, image_query_rows, image_output_grad, image_key_rows, image_value_codes)
    slots = to_groups(slots)
    own, key_flat = join_slots(slots)
    pieces, mine, other = gather_rows(own, key_flat)
    stats, qa, ga, ka, va = row_stats(
        place,
        timestep_group,
        timestep,
        value_step_sizes,
        pieces,
        mine,
        other,
        text_query_rows,
        text_output_grad,
        text_key_rows,
        text_value_rows,
    )

    input_rows, stats = lax.optimization_barrier((image_input_rows, stats))
    stats = lax.all_to_all(stats, "z", split_axis=0, concat_axis=0, tiled=True)
    more = to_groups(pack_more(place, input_rows, value_fraction, adapter_down_weight.T))
    stats, more = lax.optimization_barrier((stats, more))

    own_q, two_up, two_down, near_up, near_down, far, *chunks = row_grads(
        place, qa, ga, ka, va, stats
    )
    keep_v, send_v, keep_k, send_k = chunks
    sum_v = keep_v + flip(send_v, "core", 1).astype(F32)
    low_v, near_up, near_down, send_k = lax.optimization_barrier(
        (sum_v.astype(BF16), near_up, near_down, send_k)
    )
    sum_k = keep_k + flip(send_k, "core", 1).astype(F32)

    arrived = [shift(low_v[d], "x", d) for d in range(1, 4)]
    from_below = shift(near_up, "z", 1)
    from_above = shift(near_down, "z", -1)
    arrived, from_below, from_above, low_k = lax.optimization_barrier(
        (arrived, from_below, from_above, sum_k.astype(BF16))
    )
    dv_slots, low_part, up_part, steps_part = value_terms(
        place, sum_v[0], *arrived, key_flat, *more, adapter_up_weight
    )
    low_part, far = lax.optimization_barrier((low_part, far))
    low_parts = [shift(low_part, "head", d) for d in range(1, GROUPS)]
    far_below = shift(far, "z", 2)
    two_up = two_up + from_below[:CHUNK].astype(F32) + far_below.astype(F32)
    two_down = two_down + from_above[:CHUNK].astype(F32)
    dq_own = own_q + from_below[CHUNK:].astype(F32) + from_above[CHUNK:].astype(F32)

    two_up, two_down = two_up.astype(BF16), two_down.astype(BF16)
    keep_a, send_a = adapter_terms(place, low_part, *low_parts, *more, up_part, steps_part)
    total_k = sum_k[0]
    for d in range(1, 4):
        total_k = total_k + shift(low_k[d], "x", d).astype(F32)
    total_k = total_k.astype(BF16)

    sum_a = keep_a + flip(send_a, "core", 1)
    low_a, two_up, two_down = lax.optimization_barrier((sum_a.astype(BF16), two_up, two_down))
    arrived_a = [shift(low_a[d], "x", d) for d in range(1, 4)]
    two_below = shift(two_up, "z", 2)
    two_above = shift(two_down, "z", -2)
    arrived_a, two_below, two_above = lax.optimization_barrier((arrived_a, two_below, two_above))
    total = sum_a[0]
    for part in arrived_a:
        total = total + part.astype(F32)
    dq_own = (dq_own + two_below.astype(F32) + two_above.astype(F32)).astype(BF16)
    back = jnp.stack(
        [
            dq_own[:OWN].reshape(GROUPS, TOKENS, WIDTH),
            total_k[:OWN].reshape(GROUPS, TOKENS, WIDTH),
            dv_slots,
        ],
        axis=1,
    )
    terms = jnp.broadcast_to(total.astype(BF16)[None], (8, 8, LANES))
    terms, back = lax.optimization_barrier((terms, back))
    terms = lax.all_to_all(terms, "z", split_axis=0, concat_axis=0, tiled=True)
    terms, returned = lax.optimization_barrier((terms, from_groups(back)))
    total = jnp.sum(terms.astype(F32), axis=0).astype(BF16)
    dq_img, dk_img, image_value_grad, dq_txt, dk_txt, dv_txt = place_rows(
        place, returned, image_value_codes, dq_own, total_k
    )
    by_x = jnp.stack([total] + [shift(total, "x", d) for d in range(1, 4)])
    by_group = jnp.stack([by_x] + [shift(by_x, "head", d) for d in range(1, GROUPS)])
    other = flip(by_group, "core", 1)
    grad_down, grad_up, grad_steps = place_totals(
        place, timestep_group, timestep, by_group, other
    )
    return (
        dq_img,
        dk_img,
        image_value_grad,
        dq_txt,
        dk_txt,
        dv_txt,
        grad_down.T,
        grad_up,
        grad_steps,
    )


def solution(mesh):
    fine = Mesh(mesh.devices.reshape(4, 8, 2, 4), ("x", "z", "core", "head"))
    seq = ("x", "z", "core")
    tokens = P(seq + ("head",), None)
    heads = P(None, "head")
    return jax.shard_map(
        on_device,
        mesh=fine,
        in_specs=(
            tokens,
            P(),
            P(),
            tokens,
            tokens,
            tokens,
            tokens,
            P(),
            P(),
            P(),
            tokens,
            heads,
            heads,
            heads,
            heads,
        ),
        out_specs=(
            tokens,
            tokens,
            tokens,
            P(seq, "head"),
            P(seq, "head"),
            P(seq, "head"),
            P(),
            P(),
            P(),
        ),
        check_vma=False,
    )
```

```python
import functools
import math

import jax
import jax.numpy as jnp
from jax import lax
from jax.experimental import pallas as pl
from jax.experimental.pallas import tpu as pltpu
from jax.sharding import Mesh
from jax.sharding import PartitionSpec as P

HEAD_SIZE = 128
QMAX = 127
UNSCALE = 0.0078125
SCALE = HEAD_SIZE ** -0.5
SCALE_LOG2 = SCALE * math.log2(math.e)

OWN = 128
IMG_ROWS = 1024
TXT_ROWS = 64
ROWS = IMG_ROWS + TXT_ROWS
HEADS = 3
WIDTH = HEADS * HEAD_SIZE
TOKENS = 32
GROUPS = 4
RANK = 64
DOWN = 768
LANES = 1280
LINE = 1152
CHUNK = OWN + 16
TILE = 512

BF16 = jnp.bfloat16
F32 = jnp.float32
NT = (((1,), (1,)), ((), ()))
NN = (((1,), (0,)), ((), ()))
TN = (((0,), (0,)), ((), ()))


def dot(a, b, dims):
    return lax.dot_general(a, b, dims, preferred_element_type=F32)


def shift(rows, axis, step):
    size = lax.axis_size(axis)
    return lax.ppermute(rows, axis, [(i, (i + step) % size) for i in range(size)])


def flip(rows, axis, bit):
    size = lax.axis_size(axis)
    return lax.ppermute(rows, axis, [(i, i ^ bit) for i in range(size)])


def smem():
    return pl.BlockSpec(memory_space=pltpu.SMEM)


def vmem():
    return pl.BlockSpec(memory_space=pltpu.VMEM)


def params():
    return pltpu.CompilerParams(vmem_limit_bytes=56 << 20)


def shape(dims, dtype=BF16):
    return jax.ShapeDtypeStruct(dims, dtype)


def wrap(index, size):
    return lax.rem(index, size)


def columns(group, width):
    return pl.ds(pl.multiple_of(group * width, HEAD_SIZE), width)


def pack_kernel(place, q, g, k, codes, *outs):
    y = place[3]
    for d in range(GROUPS):
        at = columns(wrap(y + d, GROUPS), WIDTH)
        outs[d][0] = q[:, at]
        outs[d][1] = g[:, at]
        outs[d][2] = k[:, at]
        outs[d][3] = codes[:, at].astype(F32).astype(BF16)


def pack_rows(place, *rows):
    return pl.pallas_call(
        pack_kernel,
        in_specs=[smem()] + [vmem()] * 4,
        out_specs=[vmem()] * GROUPS,
        out_shape=[shape((4, TOKENS, WIDTH))] * GROUPS,
        name="pack_rows",
        compiler_params=params(),
    )(place, *rows)


def join_kernel(s0, s1, s2, s3, rows, keys):
    for d, slot in enumerate((s0, s1, s2, s3)):
        rows[d * TOKENS:(d + 1) * TOKENS] = slot[0]
        rows[OWN + d * TOKENS:OWN + (d + 1) * TOKENS] = slot[1]
        keys[2 * d * TOKENS:(2 * d + 1) * TOKENS] = slot[2]
        keys[(2 * d + 1) * TOKENS:(2 * d + 2) * TOKENS] = slot[3]


def join_slots(slots):
    return pl.pallas_call(
        join_kernel,
        in_specs=[vmem()] * GROUPS,
        out_specs=[vmem()] * 2,
        out_shape=[shape((2 * OWN, WIDTH))] * 2,
        name="join_slots",
        compiler_params=params(),
    )(*slots)


def pack_more_kernel(place, x, fraction, down_t, *outs):
    y = place[3]
    low = dot(x[...], down_t[...], NT).astype(BF16)
    blank = jnp.zeros((TOKENS, HEAD_SIZE - RANK), BF16)
    for d in range(GROUPS):
        group = wrap(y + d, GROUPS)
        outs[d][:, 0:DOWN] = x[:, columns(group, DOWN)]
        outs[d][:, DOWN:DOWN + WIDTH] = fraction[:, columns(group, WIDTH)]
        outs[d][:, DOWN + WIDTH:LANES] = jnp.concatenate([low, blank], axis=1)


def pack_more(place, *rows):
    return pl.pallas_call(
        pack_more_kernel,
        in_specs=[smem()] + [vmem()] * 3,
        out_specs=[vmem()] * GROUPS,
        out_shape=[shape((TOKENS, LANES))] * GROUPS,
        name="pack_more",
        compiler_params=params(),
    )(place, *rows)


def query_tiles():
    return [(s, TILE) for s in range(0, IMG_ROWS, TILE)] + [(IMG_ROWS, TXT_ROWS)]


PIECES = 9


def place_pieces(qa, ga, pieces, z):
    for piece, step in zip(pieces[:7], (0, 7, 6, 5, 1, 2, 3)):
        start = pl.multiple_of(wrap(z + step, 8) * OWN, OWN)
        qa[pl.ds(start, OWN)] = piece[0:OWN]
        ga[pl.ds(start, OWN)] = piece[OWN:2 * OWN]
    start = pl.multiple_of(wrap(z + 4, 8) * OWN, OWN)
    qa[pl.ds(start, OWN)] = pieces[7][...]
    ga[pl.ds(start, OWN)] = pieces[8][...]


def query_text(text, place):
    row = lax.broadcasted_iota(jnp.int32, (TXT_ROWS, 512), 0)
    column = lax.broadcasted_iota(jnp.int32, (TXT_ROWS, 512), 1)
    wanted = lax.shift_right_logical(row, 3) * 16 + lax.bitwise_and(row, 7)
    pick = jnp.where(column == wanted + place[0] * 128 + place[2] * 8, 1.0, 0.0).astype(BF16)
    return dot(pick, text[...], NN).astype(BF16)


def key_text(text, place):
    row = lax.broadcasted_iota(jnp.int32, (TXT_ROWS, 512), 0)
    column = lax.broadcasted_iota(jnp.int32, (TXT_ROWS, 512), 1)
    block = lax.shift_right_logical(row, 4) * 128 + lax.bitwise_and(row, 15)
    pick = jnp.where(column == block + place[1] * 16, 1.0, 0.0).astype(BF16)
    return dot(pick, text[...], NN).astype(BF16)


def rows_spec(rows):
    return pl.BlockSpec((rows, HEAD_SIZE), lambda h: (0, h))


def line_spec(copies):
    return pl.BlockSpec((copies, 2, LINE), lambda h: (0, 0, h))


def cost(matmuls, moved):
    return pl.CostEstimate(
        flops=2 * matmuls * HEADS * ROWS * ROWS * HEAD_SIZE,
        bytes_accessed=moved << 20,
        transcendentals=HEADS * ROWS * ROWS,
    )


def chunk_spec(rows):
    return pl.BlockSpec((4, rows, HEAD_SIZE), lambda h: (0, 0, h))


def stat_kernel(place, group, timestep, sizes, *refs):
    pieces = refs[:PIECES]
    mine, other, qt, gt, kt, vt, out, qa, ga, ka, va = refs[PIECES:]
    x, c = place[0], place[2]
    step = sizes[group[timestep[0]], place[3] * HEADS + pl.program_id(0)]
    place_pieces(qa, ga, pieces, place[1])
    qa[IMG_ROWS:ROWS] = query_text(qt, place)
    ga[IMG_ROWS:ROWS] = query_text(gt, place)
    ka[IMG_ROWS:ROWS] = key_text(kt, place)
    va[IMG_ROWS:ROWS] = key_text(vt, place)
    for i, e in enumerate((0, 3, 1, 2)):
        for core, part in ((c, mine), (1 - c, other)):
            start = pl.multiple_of((wrap(x + e, 4) * 2 + core) * OWN, OWN)
            pairs = part[i * 2 * OWN:(i + 1) * 2 * OWN].reshape(GROUPS, 2, TOKENS, HEAD_SIZE)
            ka[pl.ds(start, OWN)] = pairs[:, 0].reshape(OWN, HEAD_SIZE)
            codes = pairs[:, 1].reshape(OWN, HEAD_SIZE).astype(F32)
            va[pl.ds(start, OWN)] = (codes * step).astype(BF16)
    for s, n in query_tiles():
        st = dot(ka[...], qa[s:s + n], NT)
        m = jnp.max(st, axis=0, keepdims=True)
        e = jnp.exp2((st - m) * SCALE_LOG2)
        l = jnp.sum(e, axis=0, keepdims=True)
        dp = dot(va[...], ga[s:s + n], NT)
        w = jnp.sum(e * dp, axis=0, keepdims=True)
        lines = jnp.concatenate([m * SCALE_LOG2 + jnp.log2(l), w / l], axis=0)
        out[:, :, s:s + n] = jnp.broadcast_to(lines[None], (8, 2, n))
    out[:, :, ROWS:LINE] = jnp.zeros((8, 2, LINE - ROWS), F32)


def row_stats(place, group, timestep, sizes, pieces, *operands):
    return pl.pallas_call(
        stat_kernel,
        grid=(HEADS,),
        in_specs=[smem()] * 4
        + [rows_spec(2 * OWN)] * 7
        + [rows_spec(OWN)] * 2
        + [rows_spec(8 * OWN)] * 2
        + [rows_spec(512)] * 4,
        out_specs=[line_spec(8)] + [rows_spec(ROWS)] * 4,
        out_shape=[shape((8, 2, HEADS * LINE), F32)] + [shape((ROWS, WIDTH))] * 4,
        name="row_stats",
        compiler_params=params(),
        cost_estimate=cost(2, 8),
    )(place, group, timestep, sizes, *pieces, *operands)


def grad_kernel(place, qa, ga, ka, va, stats, *refs):
    outs, (keep_v, send_v, keep_k, send_k, p_s, d_s, v_s, k_s, q_s) = refs[:6], refs[6:]
    x, z, c = place[0], place[1], place[2]
    logs, parts = stats[:, 0], stats[:, 1]
    m = jnp.max(logs, axis=0, keepdims=True)
    e = jnp.exp2(logs - m)
    l = jnp.sum(e, axis=0, keepdims=True)
    log = m + jnp.log2(l)
    delta = jnp.sum(e * parts, axis=0, keepdims=True) / l
    for s, n in query_tiles():
        st = dot(ka[...], qa[s:s + n], NT)
        p = jnp.exp2(st * SCALE_LOG2 - log[:, s:s + n])
        dp = dot(va[...], ga[s:s + n], NT)
        p_s[:, s:s + n] = p.astype(BF16)
        d_s[:, s:s + n] = (p * (dp - delta[:, s:s + n])).astype(BF16)
    v_s[...] = dot(p_s[...], ga[...], NN)
    k_s[...] = dot(d_s[...], qa[...], NN) * SCALE
    q_s[...] = dot(d_s[...], ka[...], TN) * SCALE
    blank = jnp.zeros((8, HEAD_SIZE), F32)
    own, two_up, two_down, near_up, near_down, far = outs
    for to, first, step in (
        (own, 0, 0),
        (two_up, 0, 2),
        (two_down, 0, 6),
        (near_up, 0, 3),
        (near_up, CHUNK, 1),
        (near_down, 0, 5),
        (near_down, CHUNK, 7),
        (far, 0, 4),
    ):
        chunk = wrap(z + step, 8)
        rows = pl.ds(pl.multiple_of(chunk * OWN, OWN), OWN)
        text = pl.ds(pl.multiple_of(IMG_ROWS + chunk * 8, 8), 8)
        to[first:first + OWN] = q_s[rows].astype(to.dtype)
        tail = jnp.concatenate([q_s[text], blank], axis=0)
        to[first + OWN:first + CHUNK] = tail.astype(to.dtype)
    for d in range(4):
        for core, to_v, to_k in ((c, keep_v, keep_k), (1 - c, send_v, send_k)):
            chunk = wrap(x + d, 4) * 2 + core
            rows = pl.ds(pl.multiple_of(chunk * OWN, OWN), OWN)
            text = pl.ds(pl.multiple_of(IMG_ROWS + chunk * 8, 8), 8)
            to_v[d] = v_s[rows].astype(to_v.dtype)
            to_k[d, 0:OWN] = k_s[rows].astype(to_k.dtype)
            both = jnp.concatenate([k_s[text], v_s[text]], axis=0)
            to_k[d, OWN:CHUNK] = both.astype(to_k.dtype)


def row_grads(place, *operands):
    return pl.pallas_call(
        grad_kernel,
        grid=(HEADS,),
        in_specs=[smem()] + [rows_spec(ROWS)] * 4 + [line_spec(8)],
        out_specs=[rows_spec(CHUNK)] * 3
        + [rows_spec(2 * CHUNK)] * 2
        + [rows_spec(CHUNK)]
        + [chunk_spec(OWN)] * 2
        + [chunk_spec(CHUNK)] * 2,
        out_shape=[shape((CHUNK, WIDTH), F32)] * 3
        + [shape((2 * CHUNK, WIDTH))] * 2
        + [shape((CHUNK, WIDTH))]
        + [
            shape((4, OWN, WIDTH), F32),
            shape((4, OWN, WIDTH)),
            shape((4, CHUNK, WIDTH), F32),
            shape((4, CHUNK, WIDTH)),
        ],
        scratch_shapes=[pltpu.VMEM((ROWS, ROWS), BF16)] * 2
        + [pltpu.VMEM((ROWS, HEAD_SIZE), F32)] * 3,
        name="row_grads",
        compiler_params=params(),
        cost_estimate=cost(5, 12),
    )(place, *operands)


def value_kernel(place, own, r1, r2, r3, codes, m0, m1, m2, m3, up, dv, low, up_part, steps):
    total = own[...]
    for part in (r1, r2, r3):
        total = total + part[...].astype(F32)
    dv_quant = total.astype(BF16)
    dv[...] = dv_quant.reshape(GROUPS, TOKENS, WIDTH)
    pairs = codes[...].reshape(GROUPS, 2, TOKENS, WIDTH)
    code = pairs[:, 1].reshape(OWN, WIDTH).astype(F32)
    inside = jnp.abs(code) < QMAX
    rounded = dv_quant.astype(F32)
    image_grad = jnp.where(inside, rounded, 0.0).astype(BF16)
    up_own = up[:, columns(place[3], WIDTH)]
    low[...] = dot(image_grad, up_own, NT).astype(BF16)
    more = (m0, m1, m2, m3)
    low_input = jnp.concatenate([m[:, DOWN + WIDTH:DOWN + WIDTH + RANK] for m in more], axis=0)
    fraction = jnp.concatenate([m[:, DOWN:DOWN + WIDTH] for m in more], axis=0).astype(F32)
    up_part[...] = dot(low_input, image_grad, TN)
    terms = rounded * jnp.where(inside, -fraction, code)
    sums = jnp.sum(terms, axis=0, keepdims=True)
    lane = lax.broadcasted_iota(jnp.int32, (8, HEAD_SIZE), 1)
    row = lax.broadcasted_iota(jnp.int32, (8, HEAD_SIZE), 0)
    found = jnp.zeros((8, HEAD_SIZE), F32)
    for h in range(HEADS):
        head_sum = jnp.sum(sums[:, h * HEAD_SIZE:(h + 1) * HEAD_SIZE], axis=1, keepdims=True)
        found = found + jnp.where((lane == h) & (row == 0), head_sum, 0.0)
    steps[...] = found


def value_terms(place, *operands):
    return pl.pallas_call(
        value_kernel,
        in_specs=[smem()] + [vmem()] * 10,
        out_specs=[vmem()] * 4,
        out_shape=[
            shape((GROUPS, TOKENS, WIDTH)),
            shape((OWN, RANK)),
            shape((RANK, WIDTH), F32),
            shape((8, HEAD_SIZE), F32),
        ],
        name="value_terms",
        compiler_params=params(),
    )(place, *operands)


def adapter_kernel(place, low0, low1, low2, low3, m0, m1, m2, m3, up_part, steps, keep, send, whole):
    x, c = place[0], place[2]
    total = low0[...].astype(F32)
    for d, part in ((1, low1), (2, low2), (3, low3)):
        cut = (GROUPS - d) * TOKENS
        total = total + jnp.concatenate([part[cut:], part[:cut]], axis=0).astype(F32)
    x_rows = jnp.concatenate([m[:, 0:DOWN] for m in (m0, m1, m2, m3)], axis=0)
    whole[:, 0:DOWN] = dot(total.astype(BF16), x_rows, TN)
    whole[:, DOWN:DOWN + WIDTH] = up_part[...]
    whole[:, DOWN + WIDTH:LANES] = jnp.zeros((RANK, HEAD_SIZE), F32)
    whole[0:8, DOWN + WIDTH:LANES] = steps[...]
    for d in range(4):
        for core, to in ((c, keep), (1 - c, send)):
            start = (core * 4 + wrap(x + d, 4)) * 8
            to[d] = whole[pl.ds(pl.multiple_of(start, 8), 8)].astype(to.dtype)


def adapter_terms(place, *operands):
    return pl.pallas_call(
        adapter_kernel,
        in_specs=[smem()] + [vmem()] * 10,
        out_specs=[vmem()] * 2,
        out_shape=[shape((4, 8, LANES), F32), shape((4, 8, LANES), F32)],
        scratch_shapes=[pltpu.VMEM((RANK, LANES), F32)],
        name="adapter_terms",
        compiler_params=params(),
    )(place, *operands)


def place_kernel(place, group_table, timestep, mine, other, down_t, up, steps):
    x, c, y = place[0], place[2], place[3]
    slot_row = lax.broadcasted_iota(jnp.int32, (8, HEAD_SIZE), 0) == group_table[timestep[0]]
    lane = lax.broadcasted_iota(jnp.int32, (8, HEAD_SIZE), 1)
    row = lax.broadcasted_iota(jnp.int32, (8, HEAD_SIZE), 0)
    found = jnp.zeros((1, HEAD_SIZE), F32)
    for e in range(GROUPS):
        group = wrap(y + GROUPS - e, GROUPS)
        for core, part in ((c, mine), (1 - c, other)):
            for d in range(4):
                index = core * 4 + wrap(x + 4 - d, 4)
                rows = pl.ds(pl.multiple_of(index * 8, 8), 8)
                tile = part[e, d].astype(F32) * UNSCALE
                down_t[rows, columns(group, DOWN)] = tile[:, 0:DOWN]
                up[rows, columns(group, WIDTH)] = tile[:, DOWN:DOWN + WIDTH]
                last = tile[:, DOWN + WIDTH:LANES]
                for h in range(HEADS):
                    value = jnp.sum(jnp.where((lane == h) & (row == 0), last, 0.0), axis=0, keepdims=True)
                    value = jnp.sum(value, axis=1, keepdims=True)
                    hit = (lane[0:1] == group * HEADS + h) & (index == 0)
                    found = found + jnp.where(hit, value, 0.0)
    steps[...] = jnp.where(slot_row, found * QMAX ** -0.5, 0.0)[:, 0:GROUPS * HEADS]


def place_totals(place, group_table, timestep, mine, other):
    return pl.pallas_call(
        place_kernel,
        in_specs=[smem()] * 3 + [vmem()] * 2,
        out_specs=[vmem()] * 3,
        out_shape=[
            shape((RANK, GROUPS * DOWN), F32),
            shape((RANK, GROUPS * WIDTH), F32),
            shape((8, GROUPS * HEADS), F32),
        ],
        name="place_totals",
        compiler_params=params(),
    )(place, group_table, timestep, mine, other)


def place_rows_kernel(place, *refs):
    pieces, (codes, q_tail, k_tail, dq, dk, dv, q_txt, k_txt, v_txt) = refs[:GROUPS], refs[GROUPS:]
    y = place[3]
    q_txt[...] = q_tail[OWN:OWN + 16].astype(F32)[0:8].astype(BF16)
    tail = k_tail[OWN:OWN + 16].astype(F32)
    k_txt[...] = tail[0:8].astype(BF16)
    v_txt[...] = tail[8:16].astype(BF16)
    for d in range(GROUPS):
        at = columns(wrap(y + d, GROUPS), WIDTH)
        dq[:, at] = pieces[d][0]
        dk[:, at] = pieces[d][1]
        inside = jnp.abs(codes[:, at]) < QMAX
        value = pieces[d][2].astype(F32)
        dv[:, at] = jnp.where(inside, value, 0.0).astype(BF16)


def place_rows(place, pieces, codes, q_tail, k_tail):
    return pl.pallas_call(
        place_rows_kernel,
        in_specs=[smem()] + [vmem()] * (GROUPS + 3),
        out_specs=[vmem()] * 6,
        out_shape=[shape((TOKENS, GROUPS * WIDTH))] * 3 + [shape((8, WIDTH))] * 3,
        name="place_rows",
        compiler_params=params(),
    )(place, *pieces, codes, q_tail, k_tail)


def gather_rows(rows, keys):
    half = rows.shape[0] // 2
    up = [shift(rows, "z", step) for step in (2, 1)]
    down = [shift(rows, "z", -step) for step in (2, 1)]
    left, right = shift(keys, "x", 1), shift(keys, "x", -1)
    first, second = shift(left[:half], "x", 1), shift(right[half:], "x", -1)
    up, down, left, right, first, second = lax.optimization_barrier(
        (up, down, left, right, first, second)
    )
    up3, down3 = shift(up[0], "z", 1), shift(down[0], "z", -1)
    up4, down4 = shift(up[0][:half], "z", 2), shift(down[0][half:], "z", -2)
    mine = jnp.concatenate([keys, left, right, first, second], axis=0)
    pieces = [rows, up[1], up[0], up3, down[1], down[0], down3, up4, down4]
    return pieces, mine, flip(mine, "core", 1)


def to_groups(slots):
    return [slots[0]] + [shift(slots[d], "head", d) for d in range(1, GROUPS)]


def from_groups(slots):
    return [slots[0]] + [shift(slots[d], "head", -d) for d in range(1, GROUPS)]


def on_device(
    image_input_rows,
    adapter_down_weight,
    adapter_up_weight,
    image_query_rows,
    image_key_rows,
    image_value_codes,
    value_fraction,
    value_step_sizes,
    timestep_group,
    timestep,
    image_output_grad,
    text_query_rows,
    text_key_rows,
    text_value_rows,
    text_output_grad,
):
    x_index, z_index = lax.axis_index("x"), lax.axis_index("z")
    core_index, group_index = lax.axis_index("core"), lax.axis_index("head")
    place = jnp.stack([x_index, z_index, core_index, group_index]).astype(jnp.int32)

    slots = pack_rows(place, image_query_rows, image_output_grad, image_key_rows, image_value_codes)
    slots = to_groups(slots)
    own, key_flat = join_slots(slots)
    pieces, mine, other = gather_rows(own, key_flat)
    stats, qa, ga, ka, va = row_stats(
        place,
        timestep_group,
        timestep,
        value_step_sizes,
        pieces,
        mine,
        other,
        text_query_rows,
        text_output_grad,
        text_key_rows,
        text_value_rows,
    )

    input_rows, stats = lax.optimization_barrier((image_input_rows, stats))
    stats = lax.all_to_all(stats, "z", split_axis=0, concat_axis=0, tiled=True)
    more = to_groups(pack_more(place, input_rows, value_fraction, adapter_down_weight.T))
    stats, more = lax.optimization_barrier((stats, more))

    own_q, two_up, two_down, near_up, near_down, far, *chunks = row_grads(
        place, qa, ga, ka, va, stats
    )
    keep_v, send_v, keep_k, send_k = chunks
    sum_v = keep_v + flip(send_v, "core", 1).astype(F32)
    low_v, near_up, near_down, send_k = lax.optimization_barrier(
        (sum_v.astype(BF16), near_up, near_down, send_k)
    )
    sum_k = keep_k + flip(send_k, "core", 1).astype(F32)

    arrived = [shift(low_v[d], "x", d) for d in range(1, 4)]
    from_below = shift(near_up, "z", 1)
    from_above = shift(near_down, "z", -1)
    arrived, from_below, from_above, low_k = lax.optimization_barrier(
        (arrived, from_below, from_above, sum_k.astype(BF16))
    )
    dv_slots, low_part, up_part, steps_part = value_terms(
        place, sum_v[0], *arrived, key_flat, *more, adapter_up_weight
    )
    low_part, far = lax.optimization_barrier((low_part, far))
    low_parts = [shift(low_part, "head", d) for d in range(1, GROUPS)]
    far_below = shift(far, "z", 2)
    two_up = two_up + from_below[:CHUNK].astype(F32) + far_below.astype(F32)
    two_down = two_down + from_above[:CHUNK].astype(F32)
    dq_own = own_q + from_below[CHUNK:].astype(F32) + from_above[CHUNK:].astype(F32)

    two_up, two_down = two_up.astype(BF16), two_down.astype(BF16)
    keep_a, send_a = adapter_terms(place, low_part, *low_parts, *more, up_part, steps_part)
    total_k = sum_k[0]
    for d in range(1, 4):
        total_k = total_k + shift(low_k[d], "x", d).astype(F32)
    total_k = total_k.astype(BF16)

    sum_a = keep_a + flip(send_a, "core", 1)
    low_a, two_up, two_down = lax.optimization_barrier((sum_a.astype(BF16), two_up, two_down))
    arrived_a = [shift(low_a[d], "x", d) for d in range(1, 4)]
    two_below = shift(two_up, "z", 2)
    two_above = shift(two_down, "z", -2)
    arrived_a = lax.optimization_barrier(arrived_a)
    total = sum_a[0]
    for part in arrived_a:
        total = total + part.astype(F32)
    dq_own = (dq_own + two_below.astype(F32) + two_above.astype(F32)).astype(BF16)
    back = jnp.stack(
        [
            dq_own[:OWN].reshape(GROUPS, TOKENS, WIDTH),
            total_k[:OWN].reshape(GROUPS, TOKENS, WIDTH),
            dv_slots,
        ],
        axis=1,
    )
    terms = jnp.broadcast_to(total.astype(BF16)[None], (8, 8, LANES))
    terms = lax.all_to_all(terms, "z", split_axis=0, concat_axis=0, tiled=True)
    terms, returned = lax.optimization_barrier((terms, from_groups(back)))
    total = jnp.sum(terms.astype(F32), axis=0).astype(BF16)
    dq_img, dk_img, image_value_grad, dq_txt, dk_txt, dv_txt = place_rows(
        place, returned, image_value_codes, dq_own, total_k
    )
    by_x = jnp.stack([total] + [shift(total, "x", d) for d in range(1, 4)])
    by_group = jnp.stack([by_x] + [shift(by_x, "head", d) for d in range(1, GROUPS)])
    other = flip(by_group, "core", 1)
    grad_down, grad_up, grad_steps = place_totals(
        place, timestep_group, timestep, by_group, other
    )
    return (
        dq_img,
        dk_img,
        image_value_grad,
        dq_txt,
        dk_txt,
        dv_txt,
        grad_down.T,
        grad_up,
        grad_steps,
    )


def solution(mesh):
    fine = Mesh(mesh.devices.reshape(4, 8, 2, 4), ("x", "z", "core", "head"))
    seq = ("x", "z", "core")
    tokens = P(seq + ("head",), None)
    heads = P(None, "head")
    return jax.shard_map(
        on_device,
        mesh=fine,
        in_specs=(
            tokens,
            P(),
            P(),
            tokens,
            tokens,
            tokens,
            tokens,
            P(),
            P(),
            P(),
            tokens,
            heads,
            heads,
            heads,
            heads,
        ),
        out_specs=(
            tokens,
            tokens,
            tokens,
            P(seq, "head"),
            P(seq, "head"),
            P(seq, "head"),
            P(),
            P(),
            P(),
        ),
        check_vma=False,
    )
```
